32 devices in a mesh: pipe: 4 (over y, x), ctx: 8 (over z, core).
Axes of the slice: x: 2, y: 2, z: 4, core: 2. Of those that a mesh axis runs over, the one named last changes fastest.
Arguments:
- queries: bfloat16 [4, 4096, 1024], P('pipe', 'ctx'), may hold values from -14 to 14
- keys: bfloat16 [4, 4096, 128], P('pipe', 'ctx'), may hold values from -14 to 14
- values: bfloat16 [4, 4096, 128], P('pipe', 'ctx'), may hold values from -6 to 6
- out_grad: bfloat16 [4, 4096, 1024], P('pipe', 'ctx'), may hold values from -6 to 6
- doc_lengths: int32 [4, 8], P('pipe'), may hold values from 1 to 2048, 4096 in all within a row
- assignment: int32 [4, 8], P('pipe'), may hold values from 0 to 7, each once within a row
Outputs:
- q_grad_in: bfloat16 [4, 4096, 1024], P('pipe', 'ctx')
- k_grad_in: bfloat16 [4, 4096, 128], P('pipe', 'ctx')
- v_grad_in: bfloat16 [4, 4096, 128], P('pipe', 'ctx')
The draws below stay inside these ranges and needn't reach their ends.
Inputs may be any that keep to these rules, and one draw needn't show every extreme that they name: Each row is a permutation; device i of ctx holds the blocks assignment[s, i] and 15 - assignment[s, i] of 256 positions, in that order. `doc_lengths`: each row sums to 4096 and its largest entry is 2048.
All inputs are finite; a program needn't handle non-finite values.
Results may differ from the reference program's by a relative error of at most 0.0069.
Values may be sent and summed in bfloat16 or wider, within the bound.
A program may use at most 128 MiB of HBM per device.

```python
import math
import jax
import jax.numpy as jnp
import numpy as np
from jax import lax

BLOCK = 256
HQ = 8
HD = 128
DOCS = 8
LENGTH = 4096
MOST = 2048
SECTIONS = 4
N_CTX = 8


def draw_queries(key, part):
    drawn = jnp.clip(jax.random.normal(jax.random.fold_in(key, 21), (SECTIONS, LENGTH, HQ * HD), jnp.float32), -5.0, 5.0)
    return drawn.astype(jnp.bfloat16)


def draw_keys(key, part):
    drawn = jnp.clip(jax.random.normal(jax.random.fold_in(key, 31), (SECTIONS, LENGTH, HD), jnp.float32), -5.0, 5.0)
    return drawn.astype(jnp.bfloat16)


def level_of(own_key, dims, cuts, low, largest):
    def one(dim, parts):
        steps = jax.random.uniform(jax.random.fold_in(jax.random.fold_in(own_key, 6), dim), (parts,), jnp.float32, low / len(cuts), largest / len(cuts))
        return jnp.repeat(jnp.exp(steps), dims[dim] // parts).reshape((-1,) + (1,) * (len(dims) - dim - 1))

    factor_of = one(*cuts[0])
    for cut in cuts[1:]:
        factor_of = factor_of * one(*cut)
    return factor_of


def profile(count, total, bound, skew):
    loads = [(1 << 20) // math.isqrt(rank ** skew) + 1 for rank in range(2, count + 1)]
    surplus, given = total - bound - (count - 1), [1] * (count - 1)
    while surplus > 0:
        free = [i for i in range(count - 1) if given[i] < bound]
        pool, remaining = sum([loads[i] for i in free]), surplus
        for i in free:
            more = min(bound - given[i], max(1, remaining * loads[i] // pool), surplus)
            given[i] = given[i] + more
            surplus = surplus - more
    return np.array([bound] + given)


def ragged_sizes(own_key, amount, total, limit, skew):
    if amount == 2:
        one = jax.random.randint(own_key, (), max(1, total - limit), min(limit, total - 1) + 1)
        return jnp.stack([one, total - one])
    tallies = jnp.asarray(profile(amount, total, limit, skew), jnp.int32)
    twos = (amount - 1) // 2
    donor, receiver = tallies[1:1 + 2 * twos:2], tallies[2:2 + 2 * twos:2]
    room = jnp.minimum(donor - 1, limit - receiver)
    passed = jax.random.randint(jax.random.fold_in(own_key, 1), (twos,), 0, 1 << 20) % (room + 1)
    tallies = tallies.at[1:1 + 2 * twos:2].set(donor - passed).at[2:2 + 2 * twos:2].set(receiver + passed)
    return tallies[jax.random.permutation(jax.random.fold_in(own_key, 2), amount)]


def centred(own_key, shape, scale, reach, split=(), kind=jnp.bfloat16):
    drawn = scale * jax.random.normal(own_key, shape, jnp.float32)
    if split:
        drawn = drawn * level_of(own_key, shape, split, -0.22, 0.18)
    return jnp.clip(drawn, -reach, reach).astype(kind)


def setup_inputs(seed: int = 0) -> dict:
    arg_keys = jax.random.split(jax.random.key(seed), 7)
    queries = draw_queries(jax.random.fold_in(arg_keys[6], 71), 0)
    keys = draw_keys(jax.random.fold_in(arg_keys[6], 71), 0)
    values = centred(arg_keys[2], (SECTIONS, LENGTH, HD), 1.0, 6.0, ((0, 4), (1, 8)))
    out_grad = centred(arg_keys[3], (SECTIONS, LENGTH, HQ * HD), 1.0, 6.0, ((0, 4), (1, 8)))
    doc_lengths = jax.vmap(lambda own: ragged_sizes(own, DOCS, LENGTH, MOST, 2))(jax.random.split(arg_keys[4], SECTIONS)).reshape((SECTIONS, DOCS)).astype(jnp.int32)
    assignment = jax.vmap(lambda own: jax.random.permutation(own, N_CTX))(jax.random.split(arg_keys[5], SECTIONS)).reshape((SECTIONS, N_CTX)).astype(jnp.int32)
    return dict(queries=queries, keys=keys, values=values, out_grad=out_grad, doc_lengths=doc_lengths, assignment=assignment)


def doc_index(position, doc_starts):
    return lax.optimization_barrier(jnp.sum((position[..., None] >= doc_starts).astype(jnp.int32), axis=-1)) - 1

def section_backward(queries, keys, values, out_grad, doc_sizes, placing):
    stored_rows = jnp.arange(LENGTH, dtype=jnp.int32)
    device_of = stored_rows // (2 * BLOCK)
    half_of = stored_rows // BLOCK % 2
    own_block = placing[device_of].astype(jnp.int32)
    block_id = jnp.where(half_of == 0, own_block, 2 * N_CTX - 1 - own_block)
    position = (block_id * BLOCK + stored_rows % BLOCK).astype(jnp.int32)
    sorted_from = jnp.zeros((LENGTH,), jnp.int32).at[position].set(stored_rows)
    query_sorted = queries[sorted_from]
    key_sorted = keys[sorted_from]
    value_sorted = values[sorted_from]
    grad_sorted = out_grad[sorted_from]
    doc_starts = (jnp.cumsum(doc_sizes) - doc_sizes).astype(jnp.int32)
    doc_all = doc_index(jnp.arange(LENGTH, dtype=jnp.int32), doc_starts)
    score_scale = 1.0 / math.sqrt(HD)
    window = MOST + BLOCK

    def one_block(loop_state, block_number):
        key_acc, value_acc = loop_state
        first = (block_number * BLOCK).astype(jnp.int32)
        lowest = jnp.maximum(first - MOST, 0).astype(jnp.int32)
        query_tile = lax.dynamic_slice_in_dim(query_sorted, first, BLOCK, 0).reshape(BLOCK, HQ, HD).astype(jnp.float32)
        grad_tile = lax.dynamic_slice_in_dim(grad_sorted, first, BLOCK, 0).reshape(BLOCK, HQ, HD).astype(jnp.float32)
        key_window = lax.dynamic_slice_in_dim(key_sorted, lowest, window, 0).astype(jnp.float32)
        value_window = lax.dynamic_slice_in_dim(value_sorted, lowest, window, 0).astype(jnp.float32)
        query_pos = first + jnp.arange(BLOCK, dtype=jnp.int32)
        key_pos = lowest + jnp.arange(window, dtype=jnp.int32)
        query_doc = lax.dynamic_slice_in_dim(doc_all, first, BLOCK, 0)
        key_doc = lax.dynamic_slice_in_dim(doc_all, lowest, window, 0)
        allowed = (key_pos[None, :] <= query_pos[:, None]) & (key_doc[None, :] == query_doc[:, None])
        scores = jnp.einsum('qhd,kd->hqk', query_tile, key_window) * score_scale
        logsum = jax.nn.logsumexp(jnp.where(allowed[None], scores, -jnp.inf), axis=-1)
        softmax = jnp.where(allowed[None], jnp.exp(scores - logsum[..., None]), 0.0)
        grad_probs = jnp.einsum('qhd,kd->hqk', grad_tile, value_window)
        row_delta = lax.optimization_barrier(jnp.sum(softmax * grad_probs, axis=-1))
        grad_scores = lax.optimization_barrier((softmax * (grad_probs - row_delta[..., None])).astype(jnp.bfloat16)).astype(jnp.float32)
        softmax_low = lax.optimization_barrier(softmax.astype(jnp.bfloat16)).astype(jnp.float32)
        query_grad = jnp.einsum('hqk,kd->qhd', grad_scores, key_window) * score_scale
        key_grad = jnp.einsum('hqk,qhd->kd', grad_scores, query_tile) * score_scale
        value_grad = jnp.einsum('hqk,qhd->kd', softmax_low, grad_tile)
        key_acc = lax.dynamic_update_slice_in_dim(key_acc, lax.dynamic_slice_in_dim(key_acc, lowest, window, 0) + key_grad, lowest, 0)
        value_acc = lax.dynamic_update_slice_in_dim(value_acc, lax.dynamic_slice_in_dim(value_acc, lowest, window, 0) + value_grad, lowest, 0)
        return ((key_acc, value_acc), query_grad.reshape(BLOCK, HQ * HD))
    start_state = (jnp.zeros((LENGTH, HD), jnp.float32), jnp.zeros((LENGTH, HD), jnp.float32))
    (key_acc, value_acc), query_blocks = lax.scan(one_block, start_state, jnp.arange(2 * N_CTX, dtype=jnp.int32))
    query_all = query_blocks.reshape(LENGTH, HQ * HD)
    return (query_all[position].astype(jnp.bfloat16), key_acc[position].astype(jnp.bfloat16), value_acc[position].astype(jnp.bfloat16))

def reference(queries, keys, values, out_grad, doc_lengths, assignment):

    def per_section(section):
        return section_backward(queries[section], keys[section], values[section], out_grad[section], doc_lengths[section], assignment[section])
    query_grad, key_grad, value_grad = lax.map(per_section, jnp.arange(SECTIONS, dtype=jnp.int32))
    return (jnp.roll(query_grad, -1, axis=0), jnp.roll(key_grad, -1, axis=0), jnp.roll(value_grad, -1, axis=0))
```

```python
import math

import jax
import jax.numpy as jnp
from jax import lax
from jax.experimental import pallas as pl
from jax.experimental.pallas import tpu as pltpu
from jax.sharding import PartitionSpec as P

masked_score = -1e30
heads_together = 4


def dot_nt(a, b):
    return lax.dot_general(a, b, (((1,), (1,)), ((), ())), preferred_element_type=jnp.float32)


def dot_nn(a, b):
    return lax.dot_general(a, b, (((1,), (0,)), ((), ())), preferred_element_type=jnp.float32)


def dot_tn(a, b):
    return lax.dot_general(a, b, (((0,), (0,)), ((), ())), preferred_element_type=jnp.float32)


def attention_kernel(
    sizes_ref,
    placing_ref,
    q_ref,
    g_ref,
    kv_ref,
    dq_ref,
    dkv_ref,
    qs_ref,
    gs_ref,
    p_ref,
    dp_ref,
    tops_ref,
    dqt_ref,
    acc_ref,
    place_ref,
):
    block = q_ref.shape[0] // 2
    head_width = kv_ref.shape[1] // 2
    head_count = q_ref.shape[1] // head_width
    n_ctx = placing_ref.shape[1]
    n_docs = sizes_ref.shape[1]
    groups = head_count // heads_together
    wide = heads_together * block
    scale = 1.0 / math.sqrt(head_width)
    scale2 = scale * math.log2(math.e)
    me = lax.axis_index("ctx")

    starts = [jnp.int32(0)]
    for d in range(n_docs - 1):
        starts.append(starts[-1] + sizes_ref[0, d])
    for d in range(n_ctx):
        low = placing_ref[0, d]
        place_ref[low] = 2 * d
        place_ref[2 * n_ctx - 1 - low] = 2 * d + 1
    acc_ref[...] = jnp.zeros_like(acc_ref)
    own = placing_ref[0, me]

    def one_strip(step, carry):
        slot = step // groups
        group = step % groups
        query_block = jnp.where(slot == 0, own, 2 * n_ctx - 1 - own)
        rows = pl.ds(pl.multiple_of(slot * block, block), block)
        for h in range(heads_together):
            lanes = pl.ds(
                pl.multiple_of((group * heads_together + h) * head_width, head_width), head_width
            )
            qs_ref[h * block : (h + 1) * block, :] = q_ref[rows, lanes]
            gs_ref[h * block : (h + 1) * block, :] = g_ref[rows, lanes]
        first = query_block * block
        query_pos = first + lax.broadcasted_iota(jnp.int32, (1, block), 1)
        doc_first = jnp.zeros((1, block), jnp.int32)
        strip_first = jnp.int32(0)
        for start in starts[1:]:
            doc_first = jnp.where(query_pos >= start, start, doc_first)
            strip_first = jnp.where(first >= start, start, strip_first)
        low_block = strip_first // block
        tiles = query_block - low_block + 1
        dqt_ref[...] = jnp.zeros_like(dqt_ref)

        def forward_tile(t, state):
            top, total, weighted = state
            stored = place_ref[low_block + t]
            key_rows = pl.ds(pl.multiple_of(stored * block, block), block)
            key_tile = kv_ref[key_rows, :head_width]
            value_tile = kv_ref[key_rows, head_width:]
            key_pos = (low_block + t) * block + lax.broadcasted_iota(
                jnp.int32, (block, block), 0
            )
            allowed = (key_pos <= query_pos) & (key_pos >= doc_first)
            tops, totals, weights = [], [], []
            for h in range(heads_together):
                lanes = slice(h * block, (h + 1) * block)
                scores = dot_nt(key_tile, qs_ref[lanes, :]) * scale2
                scores = jnp.where(allowed, scores, masked_score)
                new_top = jnp.maximum(top[:, lanes], jnp.max(scores, axis=0, keepdims=True))
                probs = jnp.exp2(scores - new_top)
                grad_probs = dot_nt(value_tile, gs_ref[lanes, :])
                p_ref[t, :, lanes] = probs
                dp_ref[t, :, lanes] = grad_probs
                factor = jnp.exp2(top[:, lanes] - new_top)
                tops.append(new_top)
                totals.append(total[:, lanes] * factor + jnp.sum(probs, axis=0, keepdims=True))
                weights.append(
                    weighted[:, lanes] * factor
                    + jnp.sum(probs * grad_probs, axis=0, keepdims=True)
                )
            new_top = jnp.concatenate(tops, axis=1)
            tops_ref[t] = new_top
            return new_top, jnp.concatenate(totals, axis=1), jnp.concatenate(weights, axis=1)

        top, total, weighted = lax.fori_loop(
            0,
            tiles,
            forward_tile,
            (
                jnp.full((1, wide), masked_score, jnp.float32),
                jnp.zeros((1, wide), jnp.float32),
                jnp.zeros((1, wide), jnp.float32),
            ),
        )
        inverse = 1.0 / total
        row_delta = weighted * inverse

        def backward_tile(t, carry):
            stored = place_ref[low_block + t]
            key_rows = pl.ds(pl.multiple_of(stored * block, block), block)
            key_tile = kv_ref[key_rows, :head_width]
            factor = jnp.exp2(tops_ref[t] - top) * inverse
            softmax = p_ref[t] * factor
            grad_scores = (softmax * (dp_ref[t] - row_delta)).astype(jnp.bfloat16)
            acc_ref[key_rows, :head_width] += dot_nn(grad_scores, qs_ref[...])
            acc_ref[key_rows, head_width:] += dot_nn(softmax.astype(jnp.bfloat16), gs_ref[...])
            dqt_ref[...] += dot_tn(key_tile, grad_scores)
            return carry

        lax.fori_loop(0, tiles, backward_tile, 0)
        for h in range(heads_together):
            lanes = pl.ds(
                pl.multiple_of((group * heads_together + h) * head_width, head_width), head_width
            )
            dq_ref[rows, lanes] = (
                jnp.transpose(dqt_ref[:, h * block : (h + 1) * block]) * scale
            ).astype(jnp.bfloat16)
        return carry

    lax.fori_loop(0, 2 * groups, one_strip, 0)
    dkv_ref[:, :head_width] = (acc_ref[:, :head_width] * scale).astype(dkv_ref.dtype)
    dkv_ref[:, head_width:] = acc_ref[:, head_width:].astype(dkv_ref.dtype)


def attention_backward(doc_lengths, assignment, queries, out_grad, kv):
    rows, width = queries.shape
    length = kv.shape[0]
    block = rows // 2
    head_width = kv.shape[1] // 2
    wide = heads_together * block
    most = length // 2
    tiles = most // block + 1
    vmem = pl.BlockSpec(memory_space=pltpu.VMEM)
    smem = pl.BlockSpec(memory_space=pltpu.SMEM)
    return pl.pallas_call(
        attention_kernel,
        out_shape=(
            jax.ShapeDtypeStruct((rows, width), jnp.bfloat16),
            jax.ShapeDtypeStruct((length, 2 * head_width), jnp.bfloat16),
        ),
        in_specs=[smem, smem, vmem, vmem, vmem],
        out_specs=(vmem, vmem),
        scratch_shapes=[
            pltpu.VMEM((wide, head_width), jnp.bfloat16),
            pltpu.VMEM((wide, head_width), jnp.bfloat16),
            pltpu.VMEM((tiles, block, wide), jnp.float32),
            pltpu.VMEM((tiles, block, wide), jnp.float32),
            pltpu.VMEM((tiles, 1, wide), jnp.float32),
            pltpu.VMEM((head_width, wide), jnp.float32),
            pltpu.VMEM((length, 2 * head_width), jnp.float32),
            pltpu.SMEM((2 * assignment.shape[1],), jnp.int32),
        ],
        compiler_params=pltpu.CompilerParams(vmem_limit_bytes=60 * 1024 * 1024),
        name="attention_backward",
    )(doc_lengths, assignment, queries, out_grad, kv)


def passed_back(block):
    count = lax.axis_size("pipe")
    return lax.ppermute(block, "pipe", [((i + 1) % count, i) for i in range(count)])


def local(queries, keys, values, out_grad, doc_lengths, assignment):
    head_width = keys.shape[2]
    packed = jnp.concatenate([keys[0], values[0]], axis=1)
    kv = lax.all_gather(packed, "ctx", axis=0, tiled=True)
    query_grad, kv_part = attention_backward(doc_lengths, assignment, queries[0], out_grad[0], kv)
    query_in = passed_back(query_grad)
    kv_grad = lax.psum_scatter(kv_part, "ctx", scatter_dimension=0, tiled=True)
    kv_in = passed_back(kv_grad)
    return query_in[None], kv_in[None, :, :head_width], kv_in[None, :, head_width:]


def solution(mesh):
    return jax.shard_map(
        local,
        mesh=mesh,
        in_specs=(
            P("pipe", "ctx", None),
            P("pipe", "ctx", None),
            P("pipe", "ctx", None),
            P("pipe", "ctx", None),
            P("pipe", None),
            P("pipe", None),
        ),
        out_specs=(P("pipe", "ctx", None), P("pipe", "ctx", None), P("pipe", "ctx", None)),
        check_vma=False,
    )
```

```python
import math

import jax
import jax.numpy as jnp
from jax import lax
from jax.experimental import pallas as pl
from jax.experimental.pallas import tpu as pltpu
from jax.sharding import PartitionSpec as P

masked_score = -1e30


def dot_nt(a, b):
    return lax.dot_general(a, b, (((1,), (1,)), ((), ())), preferred_element_type=jnp.float32)


def dot_nn(a, b):
    return lax.dot_general(a, b, (((1,), (0,)), ((), ())), preferred_element_type=jnp.float32)


def dot_tn(a, b):
    return lax.dot_general(a, b, (((0,), (0,)), ((), ())), preferred_element_type=jnp.float32)


def chip_device(chip, core):
    return {"ctx": 2 * chip + core}


def greet(devices):
    barrier = pltpu.get_barrier_semaphore()
    for there, device in devices:

        @pl.when(there)
        def _():
            pl.semaphore_signal(
                barrier, inc=1, device_id=device, device_id_type=pl.DeviceIdType.MESH
            )

    count = sum(there.astype(jnp.int32) for there, device in devices)
    pl.semaphore_wait(barrier, count)


def remote(source, target, send_sem, recv_sem, device):
    return pltpu.make_async_remote_copy(
        src_ref=source,
        dst_ref=target,
        send_sem=send_sem,
        recv_sem=recv_sem,
        device_id=device,
        device_id_type=pl.DeviceIdType.MESH,
    )


def gather_kernel(
    k_ref,
    v_ref,
    q_ref,
    g_ref,
    kv_ref,
    qo_ref,
    go_ref,
    own_sem,
    line_send,
    line_recv,
    twin_send,
    twin_recv,
    swap_send,
    swap_recv,
):
    me = lax.axis_index("ctx")
    chips = kv_ref.shape[0] // 2
    half = qo_ref.shape[1]
    chip, core = me // 2, me % 2
    twin = chip_device(chip, 1 - core)
    has = (chip < chips - 1, chip > 0)
    ahead = (chip_device(chip + 1, core), chip_device(chip - 1, core))
    always = chip >= 0
    greet([(always, twin), (has[0], ahead[0]), (has[1], ahead[1])])

    own = []
    for index, ref in enumerate((k_ref, v_ref)):
        own.append(pltpu.make_async_copy(ref, kv_ref.at[me, index], own_sem.at[index]))
        own[-1].start()
    for copy in own:
        copy.wait()

    def along(way, step, hop):
        shard = 2 * (chip - step if way == 0 else chip + step) + core
        return remote(
            kv_ref.at[shard],
            kv_ref.at[shard],
            line_send.at[way, hop],
            line_recv.at[way, hop],
            ahead[way],
        )

    def across(way, step):
        shard = 2 * (chip - step if way == 0 else chip + step) + core
        return remote(
            kv_ref.at[shard],
            kv_ref.at[shard],
            twin_send.at[way, step],
            twin_recv.at[way, step],
            twin,
        )

    def arriving(way, step):
        return chip - step >= 0 if way == 0 else chip + step < chips

    for way in range(2):

        @pl.when(has[way])
        def _():
            along(way, 0, 0).start()

    across(0, 0).start()
    lanes = pl.ds(pl.multiple_of((1 - core) * half, half), half)
    swaps = [
        remote(q_ref.at[:, lanes], qo_ref, swap_send.at[0], swap_recv.at[0], twin),
        remote(g_ref.at[:, lanes], go_ref, swap_send.at[1], swap_recv.at[1], twin),
    ]
    for copy in swaps:
        copy.start()
    for step in range(1, chips):
        for way in range(2):

            @pl.when(arriving(way, step))
            def _():
                along(way, step, step - 1).wait_recv()

                @pl.when(has[way])
                def _():
                    along(way, step, step).start()

                across(way, step).start()

    for copy in swaps:
        copy.wait()
    across(0, 0).wait()
    for way in range(2):

        @pl.when(has[way])
        def _():
            along(way, 0, 0).wait_send()

    for step in range(1, chips):
        for way in range(2):

            @pl.when(arriving(way, step))
            def _():
                across(way, step).wait()

                @pl.when(has[way])
                def _():
                    along(way, step, step).wait_send()


def gather(keys, values, queries, out_grad):
    rows, width = queries.shape
    n_ctx = lax.axis_size("ctx")
    chips = n_ctx // 2
    half = width // 2
    return pl.pallas_call(
        gather_kernel,
        out_shape=(
            jax.ShapeDtypeStruct((n_ctx, 2) + keys.shape, keys.dtype),
            jax.ShapeDtypeStruct((rows, half), queries.dtype),
            jax.ShapeDtypeStruct((rows, half), queries.dtype),
        ),
        in_specs=[pl.BlockSpec(memory_space=pl.ANY)] * 4,
        out_specs=(pl.BlockSpec(memory_space=pl.ANY),) * 3,
        scratch_shapes=[
            pltpu.SemaphoreType.DMA((2,)),
            pltpu.SemaphoreType.DMA((2, chips)),
            pltpu.SemaphoreType.DMA((2, chips)),
            pltpu.SemaphoreType.DMA((2, chips)),
            pltpu.SemaphoreType.DMA((2, chips)),
            pltpu.SemaphoreType.DMA((2,)),
            pltpu.SemaphoreType.DMA((2,)),
        ],
        compiler_params=pltpu.CompilerParams(collective_id=0, has_side_effects=True),
        name="gather_blocks",
    )(keys, values, queries, out_grad)


def reduce_kernel(
    dq_ref,
    dkv_ref,
    q_in_ref,
    k_in_ref,
    v_in_ref,
    twin_ref,
    line_ref,
    sum_ref,
    twin_send,
    twin_recv,
    line_send,
    line_recv,
    query_send,
    query_recv,
    last_send,
    last_recv,
):
    me = lax.axis_index("ctx")
    stage = lax.axis_index("pipe")
    stages = lax.axis_size("pipe")
    chips = dkv_ref.shape[0] // 2
    half = dq_ref.shape[2]
    chip, core = me // 2, me % 2
    twin = chip_device(chip, 1 - core)
    has = (chip < chips - 1, chip > 0)
    ahead = (chip_device(chip + 1, core), chip_device(chip - 1, core))
    always = chip >= 0
    before = lax.rem(stage + stages - 1, stages)
    after = lax.rem(stage + 1, stages)
    greet(
        [(always, twin), (has[0], ahead[0]), (has[1], ahead[1])]
        + [
            (always, {"pipe": other, "ctx": 2 * chip + k})
            for other in (before, after)
            for k in range(2)
        ]
    )

    def crossing(z):
        return remote(
            dkv_ref.at[2 * z + 1 - core], twin_ref.at[z], twin_send.at[z], twin_recv.at[z], twin
        )

    order = []
    for z in range(chips // 2):
        order += [z, chips - 1 - z]
    for z in order:
        crossing(z).start()

    lanes = pl.ds(pl.multiple_of(core * half, half), half)

    def query_copy(k, recv_index):
        return remote(
            dq_ref.at[k],
            q_in_ref.at[:, lanes],
            query_send.at[k],
            query_recv.at[recv_index],
            {"pipe": before, "ctx": 2 * chip + k},
        )

    for k in range(2):
        query_copy(k, core).start()

    def passing(way, z):
        return remote(
            sum_ref.at[z],
            line_ref.at[way, z],
            line_send.at[way, z],
            line_recv.at[way, z],
            ahead[way],
        )

    def own_sum(z):
        return dkv_ref[2 * z + core].astype(jnp.float32) + twin_ref[z].astype(jnp.float32)

    for t in range(chips):
        for way in range(2):
            z = chips - 1 - (t - chip) if way == 0 else t - (chips - 1 - chip)
            beyond = (z <= chips - 1) & (z > chip) if way == 0 else (z >= 0) & (z < chip)

            @pl.when(beyond)
            def _():
                crossing(z).wait_recv()

                @pl.when(has[1 - way])
                def _():
                    passing(way, z).wait_recv()
                    sum_ref[z] = (own_sum(z) + line_ref[way, z].astype(jnp.float32)).astype(
                        sum_ref.dtype
                    )

                @pl.when(jnp.logical_not(has[1 - way]))
                def _():
                    sum_ref[z] = own_sum(z).astype(sum_ref.dtype)

                passing(way, z).start()

    crossing(chip).wait_recv()

    @pl.when(has[0] & has[1])
    def _():
        for way in range(2):
            passing(way, chip).wait_recv()
        sum_ref[chip] = (
            own_sum(chip)
            + line_ref[0, chip].astype(jnp.float32)
            + line_ref[1, chip].astype(jnp.float32)
        ).astype(sum_ref.dtype)

    for way in range(2):

        @pl.when(jnp.logical_not(has[way]))
        def _():
            passing(way, chip).wait_recv()
            sum_ref[chip] = (own_sum(chip) + line_ref[way, chip].astype(jnp.float32)).astype(
                sum_ref.dtype
            )

    lasts = [
        remote(
            sum_ref.at[chip, index],
            ref,
            last_send.at[index],
            last_recv.at[index],
            {"pipe": before, "ctx": me},
        )
        for index, ref in enumerate((k_in_ref, v_in_ref))
    ]
    for copy in lasts:
        copy.start()
    for k in range(2):
        query_copy(k, k).wait()
    for z in range(chips):
        crossing(z).wait_send()

        @pl.when(z > chip)
        def _():
            passing(0, z).wait_send()

        @pl.when(z < chip)
        def _():
            passing(1, z).wait_send()

    for copy in lasts:
        copy.wait()


def reduce_and_pass(dq, dkv):
    rows, half = dq.shape[1:]
    n_ctx, _, _, head_width = dkv.shape
    chips = n_ctx // 2
    part = dkv.shape[1:]
    return pl.pallas_call(
        reduce_kernel,
        out_shape=(
            jax.ShapeDtypeStruct((rows, 2 * half), dq.dtype),
            jax.ShapeDtypeStruct((rows, head_width), dq.dtype),
            jax.ShapeDtypeStruct((rows, head_width), dq.dtype),
        ),
        in_specs=[pl.BlockSpec(memory_space=pl.ANY), pl.BlockSpec(memory_space=pltpu.VMEM)],
        out_specs=(pl.BlockSpec(memory_space=pl.ANY),) * 3,
        scratch_shapes=[
            pltpu.VMEM((chips,) + part, dkv.dtype),
            pltpu.VMEM((2, chips) + part, dkv.dtype),
            pltpu.VMEM((chips,) + part, dkv.dtype),
            pltpu.SemaphoreType.DMA((chips,)),
            pltpu.SemaphoreType.DMA((chips,)),
            pltpu.SemaphoreType.DMA((2, chips)),
            pltpu.SemaphoreType.DMA((2, chips)),
            pltpu.SemaphoreType.DMA((2,)),
            pltpu.SemaphoreType.DMA((2,)),
            pltpu.SemaphoreType.DMA((2,)),
            pltpu.SemaphoreType.DMA((2,)),
        ],
        compiler_params=pltpu.CompilerParams(
            collective_id=1, has_side_effects=True, vmem_limit_bytes=40 * 1024 * 1024
        ),
        name="reduce_and_pass",
    )(dq, dkv)


def attention_kernel(
    sizes_ref,
    placing_ref,
    q_ref,
    g_ref,
    qo_ref,
    go_ref,
    kv_ref,
    dq_ref,
    dkv_ref,
    qs_ref,
    gs_ref,
    p_ref,
    dp_ref,
    tops_ref,
    dqt_ref,
    acc_ref,
    place_ref,
):
    block = q_ref.shape[0] // 2
    head_width = kv_ref.shape[3]
    head_count = q_ref.shape[1] // head_width
    n_ctx = placing_ref.shape[1]
    n_docs = sizes_ref.shape[1]
    heads = head_count // 2
    wide = heads * block
    scale = 1.0 / math.sqrt(head_width)
    scale2 = scale * math.log2(math.e)
    me = lax.axis_index("ctx")
    chip, core = me // 2, me % 2

    starts = [jnp.int32(0)]
    for d in range(n_docs - 1):
        starts.append(starts[-1] + sizes_ref[0, d])
    for d in range(n_ctx):
        low = placing_ref[0, d]
        place_ref[low] = 2 * d
        place_ref[2 * n_ctx - 1 - low] = 2 * d + 1
    acc_ref[...] = jnp.zeros_like(acc_ref)

    def one_strip(step, carry):
        owner = step // 2
        slot = step % 2
        placed = placing_ref[0, 2 * chip + owner]
        query_block = jnp.where(slot == 0, placed, 2 * n_ctx - 1 - placed)
        rows = pl.ds(pl.multiple_of(slot * block, block), block)

        @pl.when(owner == core)
        def _():
            for h in range(heads):
                lanes = pl.ds(
                    pl.multiple_of((core * heads + h) * head_width, head_width), head_width
                )
                qs_ref[h * block : (h + 1) * block, :] = q_ref[rows, lanes]
                gs_ref[h * block : (h + 1) * block, :] = g_ref[rows, lanes]

        @pl.when(owner != core)
        def _():
            for h in range(heads):
                lanes = slice(h * head_width, (h + 1) * head_width)
                qs_ref[h * block : (h + 1) * block, :] = qo_ref[rows, lanes]
                gs_ref[h * block : (h + 1) * block, :] = go_ref[rows, lanes]

        first = query_block * block
        query_pos = first + lax.broadcasted_iota(jnp.int32, (1, block), 1)
        doc_first = jnp.zeros((1, block), jnp.int32)
        strip_first = jnp.int32(0)
        for start in starts[1:]:
            doc_first = jnp.where(query_pos >= start, start, doc_first)
            strip_first = jnp.where(first >= start, start, strip_first)
        low_block = strip_first // block
        tiles = query_block - low_block + 1
        dqt_ref[...] = jnp.zeros_like(dqt_ref)

        def forward_tile(t, state):
            top, total, weighted = state
            stored = place_ref[low_block + t]
            key_rows = pl.ds(pl.multiple_of(stored % 2 * block, block), block)
            key_tile = kv_ref[stored // 2, 0, key_rows, :]
            value_tile = kv_ref[stored // 2, 1, key_rows, :]
            key_pos = (low_block + t) * block + lax.broadcasted_iota(
                jnp.int32, (block, block), 0
            )
            allowed = (key_pos <= query_pos) & (key_pos >= doc_first)
            tops, totals, weights = [], [], []
            for h in range(heads):
                lanes = slice(h * block, (h + 1) * block)
                scores = dot_nt(key_tile, qs_ref[lanes, :]) * scale2
                scores = jnp.where(allowed, scores, masked_score)
                new_top = jnp.maximum(top[:, lanes], jnp.max(scores, axis=0, keepdims=True))
                probs = jnp.exp2(scores - new_top)
                grad_probs = dot_nt(value_tile, gs_ref[lanes, :])
                p_ref[t, :, lanes] = probs
                dp_ref[t, :, lanes] = grad_probs
                factor = jnp.exp2(top[:, lanes] - new_top)
                tops.append(new_top)
                totals.append(total[:, lanes] * factor + jnp.sum(probs, axis=0, keepdims=True))
                weights.append(
                    weighted[:, lanes] * factor
                    + jnp.sum(probs * grad_probs, axis=0, keepdims=True)
                )
            new_top = jnp.concatenate(tops, axis=1)
            tops_ref[t] = new_top
            return new_top, jnp.concatenate(totals, axis=1), jnp.concatenate(weights, axis=1)

        top, total, weighted = lax.fori_loop(
            0,
            tiles,
            forward_tile,
            (
                jnp.full((1, wide), masked_score, jnp.float32),
                jnp.zeros((1, wide), jnp.float32),
                jnp.zeros((1, wide), jnp.float32),
            ),
        )
        inverse = 1.0 / total
        row_delta = weighted * inverse

        def backward_tile(t, carry):
            stored = place_ref[low_block + t]
            key_rows = pl.ds(pl.multiple_of(stored % 2 * block, block), block)
            key_tile = kv_ref[stored // 2, 0, key_rows, :]
            factor = jnp.exp2(tops_ref[t] - top) * inverse
            softmax = p_ref[t] * factor
            grad_scores = (softmax * (dp_ref[t] - row_delta)).astype(jnp.bfloat16)
            acc_ref[stored // 2, 0, key_rows, :] += dot_nn(grad_scores, qs_ref[...])
            acc_ref[stored // 2, 1, key_rows, :] += dot_nn(softmax.astype(jnp.bfloat16), gs_ref[...])
            dqt_ref[...] += dot_tn(key_tile, grad_scores)
            return carry

        lax.fori_loop(0, tiles, backward_tile, 0)
        for h in range(heads):
            dq_ref[owner, rows, h * head_width : (h + 1) * head_width] = (
                jnp.transpose(dqt_ref[:, h * block : (h + 1) * block]) * scale
            ).astype(jnp.bfloat16)
        return carry

    lax.fori_loop(0, 4, one_strip, 0)
    dkv_ref[:, 0] = (acc_ref[:, 0] * scale).astype(dkv_ref.dtype)
    dkv_ref[:, 1] = acc_ref[:, 1].astype(dkv_ref.dtype)


def attention_backward(doc_lengths, assignment, queries, out_grad, queries_other, out_grad_other, kv):
    rows, width = queries.shape
    length = kv.shape[0] * rows
    block = rows // 2
    head_width = kv.shape[3]
    wide = width // head_width // 2 * block
    most = length // 2
    tiles = most // block + 1
    vmem = pl.BlockSpec(memory_space=pltpu.VMEM)
    smem = pl.BlockSpec(memory_space=pltpu.SMEM)
    return pl.pallas_call(
        attention_kernel,
        out_shape=(
            jax.ShapeDtypeStruct((2, rows, width // 2), jnp.bfloat16),
            jax.ShapeDtypeStruct(kv.shape, jnp.bfloat16),
        ),
        in_specs=[smem, smem, vmem, vmem, vmem, vmem, vmem],
        out_specs=(vmem, vmem),
        scratch_shapes=[
            pltpu.VMEM((wide, head_width), jnp.bfloat16),
            pltpu.VMEM((wide, head_width), jnp.bfloat16),
            pltpu.VMEM((tiles, block, wide), jnp.float32),
            pltpu.VMEM((tiles, block, wide), jnp.float32),
            pltpu.VMEM((tiles, 1, wide), jnp.float32),
            pltpu.VMEM((head_width, wide), jnp.float32),
            pltpu.VMEM(kv.shape, jnp.float32),
            pltpu.SMEM((2 * assignment.shape[1],), jnp.int32),
        ],
        compiler_params=pltpu.CompilerParams(vmem_limit_bytes=60 * 1024 * 1024),
        name="attention_backward",
    )(doc_lengths, assignment, queries, out_grad, queries_other, out_grad_other, kv)


def local(queries, keys, values, out_grad, doc_lengths, assignment):
    kv, queries_other, out_grad_other = gather(keys[0], values[0], queries[0], out_grad[0])
    dq, dkv = attention_backward(
        doc_lengths, assignment, queries[0], out_grad[0], queries_other, out_grad_other, kv
    )
    query_in, key_in, value_in = reduce_and_pass(dq, dkv)
    return query_in[None], key_in[None], value_in[None]


def solution(mesh):
    return jax.shard_map(
        local,
        mesh=mesh,
        in_specs=(
            P("pipe", "ctx", None),
            P("pipe", "ctx", None),
            P("pipe", "ctx", None),
            P("pipe", "ctx", None),
            P("pipe", None),
            P("pipe", None),
        ),
        out_specs=(P("pipe", "ctx", None), P("pipe", "ctx", None), P("pipe", "ctx", None)),
        check_vma=False,
    )
```

```python
import math

import jax
import jax.numpy as jnp
from jax import lax
from jax.experimental import pallas as pl
from jax.experimental.pallas import tpu as pltpu
from jax.sharding import PartitionSpec as P

masked_score = -1e30


def dot_nt(a, b):
    return lax.dot_general(a, b, (((1,), (1,)), ((), ())), preferred_element_type=jnp.float32)


def dot_nn(a, b):
    return lax.dot_general(a, b, (((1,), (0,)), ((), ())), preferred_element_type=jnp.float32)


def dot_tn(a, b):
    return lax.dot_general(a, b, (((0,), (0,)), ((), ())), preferred_element_type=jnp.float32)


def chip_device(chip, core):
    return {"ctx": 2 * chip + core}


def greet(devices):
    barrier = pltpu.get_barrier_semaphore()
    for there, device in devices:

        @pl.when(there)
        def _():
            pl.semaphore_signal(
                barrier, inc=1, device_id=device, device_id_type=pl.DeviceIdType.MESH
            )

    count = sum(there.astype(jnp.int32) for there, device in devices)
    pl.semaphore_wait(barrier, count)


def remote(source, target, send_sem, recv_sem, device):
    return pltpu.make_async_remote_copy(
        src_ref=source,
        dst_ref=target,
        send_sem=send_sem,
        recv_sem=recv_sem,
        device_id=device,
        device_id_type=pl.DeviceIdType.MESH,
    )


def gather_kernel(
    k_ref,
    v_ref,
    q_ref,
    g_ref,
    kv_ref,
    qo_ref,
    go_ref,
    own_sem,
    line_send,
    line_recv,
    twin_send,
    twin_recv,
    swap_send,
    swap_recv,
):
    me = lax.axis_index("ctx")
    chips = kv_ref.shape[0] // 2
    half = qo_ref.shape[1]
    chip, core = me // 2, me % 2
    twin = chip_device(chip, 1 - core)
    has = (chip < chips - 1, chip > 0)
    ahead = (chip_device(chip + 1, core), chip_device(chip - 1, core))
    always = chip >= 0
    greet([(always, twin), (has[0], ahead[0]), (has[1], ahead[1])])

    sources = (k_ref, v_ref)
    own = [
        pltpu.make_async_copy(ref, kv_ref.at[me, part], own_sem.at[part])
        for part, ref in enumerate(sources)
    ]

    def shard_at(way, step):
        return 2 * (chip - step if way == 0 else chip + step) + core

    def along(way, step, hop, part):
        place = kv_ref.at[shard_at(way, step), part]
        return remote(
            sources[part] if hop == 0 and step == 0 else place,
            place,
            line_send.at[way, hop, part],
            line_recv.at[way, hop, part],
            ahead[way],
        )

    def across(way, step, part):
        place = kv_ref.at[shard_at(way, step), part]
        return remote(
            sources[part] if step == 0 else place,
            place,
            twin_send.at[way, step, part],
            twin_recv.at[way, step, part],
            twin,
        )

    def arriving(way, step):
        return chip - step >= 0 if way == 0 else chip + step < chips

    for part in range(2):
        for way in range(2):

            @pl.when(has[way])
            def _():
                along(way, 0, 0, part).start()

    for part in range(2):
        across(0, 0, part).start()
        own[part].start()
    lanes = pl.ds(pl.multiple_of((1 - core) * half, half), half)
    swaps = [
        remote(q_ref.at[:, lanes], qo_ref, swap_send.at[0], swap_recv.at[0], twin),
        remote(g_ref.at[:, lanes], go_ref, swap_send.at[1], swap_recv.at[1], twin),
    ]
    for copy in swaps:
        copy.start()
    for step in range(1, chips):
        for part in range(2):
            for way in range(2):

                @pl.when(arriving(way, step))
                def _():
                    along(way, step, step - 1, part).wait_recv()

                    @pl.when(has[way])
                    def _():
                        along(way, step, step, part).start()

                    across(way, step, part).start()

    for copy in swaps:
        copy.wait()
    for part in range(2):
        own[part].wait()
        across(0, 0, part).wait()
        for way in range(2):

            @pl.when(has[way])
            def _():
                along(way, 0, 0, part).wait_send()

    for step in range(1, chips):
        for part in range(2):
            for way in range(2):

                @pl.when(arriving(way, step))
                def _():
                    across(way, step, part).wait()

                    @pl.when(has[way])
                    def _():
                        along(way, step, step, part).wait_send()


def gather(keys, values, queries, out_grad):
    rows, width = queries.shape
    n_ctx = lax.axis_size("ctx")
    chips = n_ctx // 2
    half = width // 2
    return pl.pallas_call(
        gather_kernel,
        out_shape=(
            jax.ShapeDtypeStruct((n_ctx, 2) + keys.shape, keys.dtype),
            jax.ShapeDtypeStruct((rows, half), queries.dtype),
            jax.ShapeDtypeStruct((rows, half), queries.dtype),
        ),
        in_specs=[pl.BlockSpec(memory_space=pl.ANY)] * 4,
        out_specs=(pl.BlockSpec(memory_space=pl.ANY),) * 3,
        scratch_shapes=[
            pltpu.SemaphoreType.DMA((2,)),
            pltpu.SemaphoreType.DMA((2, chips, 2)),
            pltpu.SemaphoreType.DMA((2, chips, 2)),
            pltpu.SemaphoreType.DMA((2, chips, 2)),
            pltpu.SemaphoreType.DMA((2, chips, 2)),
            pltpu.SemaphoreType.DMA((2,)),
            pltpu.SemaphoreType.DMA((2,)),
        ],
        compiler_params=pltpu.CompilerParams(collective_id=0, has_side_effects=True),
        name="gather_blocks",
    )(keys, values, queries, out_grad)


def reduce_kernel(
    dq_ref,
    dkv_ref,
    q_in_ref,
    k_in_ref,
    v_in_ref,
    mine_ref,
    twin_ref,
    line_ref,
    sum_ref,
    twin_send,
    twin_recv,
    line_send,
    line_recv,
    query_send,
    query_recv,
    last_send,
    last_recv,
    mine_sem,
):
    me = lax.axis_index("ctx")
    stage = lax.axis_index("pipe")
    stages = lax.axis_size("pipe")
    chips = dkv_ref.shape[0] // 2
    half = dq_ref.shape[2]
    chip, core = me // 2, me % 2
    twin = chip_device(chip, 1 - core)
    has = (chip < chips - 1, chip > 0)
    ahead = (chip_device(chip + 1, core), chip_device(chip - 1, core))
    always = chip >= 0
    before = lax.rem(stage + stages - 1, stages)
    after = lax.rem(stage + 1, stages)

    def own_part(z):
        return pltpu.make_async_copy(dkv_ref.at[2 * z + core], mine_ref.at[z], mine_sem.at[z])

    order = []
    for z in range(chips // 2):
        order += [z, chips - 1 - z]
    for z in order:
        own_part(z).start()
    greet(
        [(always, twin), (has[0], ahead[0]), (has[1], ahead[1])]
        + [
            (always, {"pipe": other, "ctx": 2 * chip + k})
            for other in (before, after)
            for k in range(2)
        ]
    )

    def crossing(z):
        return remote(
            dkv_ref.at[2 * z + 1 - core], twin_ref.at[z], twin_send.at[z], twin_recv.at[z], twin
        )

    for z in order:
        crossing(z).start()

    lanes = pl.ds(pl.multiple_of(core * half, half), half)

    def query_copy(k, recv_index):
        return remote(
            dq_ref.at[k],
            q_in_ref.at[:, lanes],
            query_send.at[k],
            query_recv.at[recv_index],
            {"pipe": before, "ctx": 2 * chip + k},
        )

    for k in range(2):
        query_copy(k, core).start()

    def passing(way, z, part):
        return remote(
            sum_ref.at[z, part],
            line_ref.at[way, z, part],
            line_send.at[way, z, part],
            line_recv.at[way, z, part],
            ahead[way],
        )

    def add_up(z, part, ways):
        total = mine_ref[z, part].astype(jnp.float32) + twin_ref[z, part].astype(
            jnp.float32
        )
        for way in ways:
            total += line_ref[way, z, part].astype(jnp.float32)
        sum_ref[z, part] = total.astype(sum_ref.dtype)

    for t in range(chips - 1):
        for part in range(2):
            for way in range(2):
                z = chips - 1 - (t - chip) if way == 0 else t - (chips - 1 - chip)
                beyond = (z <= chips - 1) & (z > chip) if way == 0 else (z >= 0) & (z < chip)

                @pl.when(beyond)
                def _():
                    if part == 0:
                        own_part(z).wait()
                        crossing(z).wait_recv()

                    @pl.when(has[1 - way])
                    def _():
                        passing(way, z, part).wait_recv()
                        add_up(z, part, (way,))

                    @pl.when(jnp.logical_not(has[1 - way]))
                    def _():
                        add_up(z, part, ())

                    passing(way, z, part).start()

    own_part(chip).wait()
    crossing(chip).wait_recv()
    lasts = []
    for part, ref in enumerate((k_in_ref, v_in_ref)):

        @pl.when(has[0] & has[1])
        def _():
            for way in range(2):
                passing(way, chip, part).wait_recv()
            add_up(chip, part, (0, 1))

        for way in range(2):

            @pl.when(jnp.logical_not(has[way]))
            def _():
                passing(way, chip, part).wait_recv()
                add_up(chip, part, (way,))

        lasts.append(
            remote(
                sum_ref.at[chip, part],
                ref,
                last_send.at[part],
                last_recv.at[part],
                {"pipe": before, "ctx": me},
            )
        )
        lasts[-1].start()
    for k in range(2):
        query_copy(k, k).wait()
    for z in range(chips):
        crossing(z).wait_send()
        for part in range(2):

            @pl.when(z > chip)
            def _():
                passing(0, z, part).wait_send()

            @pl.when(z < chip)
            def _():
                passing(1, z, part).wait_send()

    for copy in lasts:
        copy.wait()


def reduce_and_pass(dq, dkv):
    rows, half = dq.shape[1:]
    n_ctx, _, _, head_width = dkv.shape
    chips = n_ctx // 2
    part = dkv.shape[1:]
    return pl.pallas_call(
        reduce_kernel,
        out_shape=(
            jax.ShapeDtypeStruct((rows, 2 * half), dq.dtype),
            jax.ShapeDtypeStruct((rows, head_width), dq.dtype),
            jax.ShapeDtypeStruct((rows, head_width), dq.dtype),
        ),
        in_specs=[pl.BlockSpec(memory_space=pl.ANY)] * 2,
        out_specs=(pl.BlockSpec(memory_space=pl.ANY),) * 3,
        scratch_shapes=[
            pltpu.VMEM((chips,) + part, dkv.dtype),
            pltpu.VMEM((chips,) + part, dkv.dtype),
            pltpu.VMEM((2, chips) + part, dkv.dtype),
            pltpu.VMEM((chips,) + part, dkv.dtype),
            pltpu.SemaphoreType.DMA((chips,)),
            pltpu.SemaphoreType.DMA((chips,)),
            pltpu.SemaphoreType.DMA((2, chips, 2)),
            pltpu.SemaphoreType.DMA((2, chips, 2)),
            pltpu.SemaphoreType.DMA((2,)),
            pltpu.SemaphoreType.DMA((2,)),
            pltpu.SemaphoreType.DMA((2,)),
            pltpu.SemaphoreType.DMA((2,)),
            pltpu.SemaphoreType.DMA((chips,)),
        ],
        compiler_params=pltpu.CompilerParams(
            collective_id=1, has_side_effects=True, vmem_limit_bytes=60 * 1024 * 1024
        ),
        name="reduce_and_pass",
    )(dq, dkv)


def attention_kernel(
    sizes_ref,
    placing_ref,
    q_ref,
    g_ref,
    qo_ref,
    go_ref,
    kv_ref,
    dq_ref,
    dkv_ref,
    qs_ref,
    gs_ref,
    s_ref,
    dp_ref,
    top_ref,
    dqt_ref,
    acc_ref,
    place_ref,
):
    block = q_ref.shape[0] // 2
    head_width = kv_ref.shape[3]
    head_count = q_ref.shape[1] // head_width
    n_ctx = placing_ref.shape[1]
    n_docs = sizes_ref.shape[1]
    heads = head_count // 2
    wide = heads * block
    scale = 1.0 / math.sqrt(head_width)
    scale2 = scale * math.log2(math.e)
    me = lax.axis_index("ctx")
    chip, core = me // 2, me % 2

    starts = [jnp.int32(0)]
    for d in range(n_docs - 1):
        starts.append(starts[-1] + sizes_ref[0, d])
    for d in range(n_ctx):
        low = placing_ref[0, d]
        place_ref[low] = 2 * d
        place_ref[2 * n_ctx - 1 - low] = 2 * d + 1
    acc_ref[...] = jnp.zeros_like(acc_ref)

    def one_strip(step, carry):
        owner = step // 2
        slot = step % 2
        placed = placing_ref[0, 2 * chip + owner]
        query_block = jnp.where(slot == 0, placed, 2 * n_ctx - 1 - placed)
        rows = pl.ds(pl.multiple_of(slot * block, block), block)

        @pl.when(owner == core)
        def _():
            for h in range(heads):
                lanes = pl.ds(
                    pl.multiple_of((core * heads + h) * head_width, head_width), head_width
                )
                qs_ref[h * block : (h + 1) * block, :] = q_ref[rows, lanes]
                gs_ref[h * block : (h + 1) * block, :] = g_ref[rows, lanes]

        @pl.when(owner != core)
        def _():
            for h in range(heads):
                lanes = slice(h * head_width, (h + 1) * head_width)
                qs_ref[h * block : (h + 1) * block, :] = qo_ref[rows, lanes]
                gs_ref[h * block : (h + 1) * block, :] = go_ref[rows, lanes]

        first = query_block * block
        query_pos = first + lax.broadcasted_iota(jnp.int32, (1, block), 1)
        doc_first = jnp.zeros((1, block), jnp.int32)
        strip_first = jnp.int32(0)
        for start in starts[1:]:
            doc_first = jnp.where(query_pos >= start, start, doc_first)
            strip_first = jnp.where(first >= start, start, strip_first)
        low_block = strip_first // block
        tiles = query_block - low_block + 1
        dqt_ref[...] = jnp.zeros_like(dqt_ref)

        last_doc = jnp.int32(0)
        for start in starts[1:]:
            last_doc = jnp.where(first + block - 1 >= start, start, last_doc)
        top_ref[...] = jnp.full(top_ref.shape, masked_score, jnp.float32)

        def tile_of(t, part):
            stored = place_ref[low_block + t]
            key_rows = pl.ds(pl.multiple_of(stored % 2 * block, block), block)
            return kv_ref[stored // 2, part, key_rows, :]

        def fold(x, combine):
            return combine(x.reshape(block // 8, 8, block), axis=0)

        def score_tile(t, carry):
            key_first = (low_block + t) * block
            key_tile = tile_of(t, 0)
            partial = (t == tiles - 1) | (key_first < last_doc)

            def scores_of(allowed):
                for h in range(heads):
                    lanes = slice(h * block, (h + 1) * block)
                    scores = dot_nt(key_tile, qs_ref[lanes, :]) * scale2
                    if allowed is not None:
                        scores = jnp.where(allowed, scores, masked_score)
                    s_ref[t, :, lanes] = scores
                    top_ref[:, lanes] = jnp.maximum(top_ref[:, lanes], fold(scores, jnp.max))

            @pl.when(partial)
            def _():
                key_pos = key_first + lax.broadcasted_iota(jnp.int32, (block, block), 0)
                scores_of((key_pos <= query_pos) & (key_pos >= doc_first))

            @pl.when(jnp.logical_not(partial))
            def _():
                scores_of(None)

            return carry

        lax.fori_loop(0, tiles, score_tile, 0)
        top = jnp.max(top_ref[...], axis=0, keepdims=True)

        def probs_tile(t, state):
            total, weighted = state
            value_tile = tile_of(t, 1)
            totals, weights = [], []
            for h in range(heads):
                lanes = slice(h * block, (h + 1) * block)
                grad_probs = dot_nt(value_tile, gs_ref[lanes, :])
                probs = jnp.exp2(s_ref[t, :, lanes] - top[:, lanes])
                dp_ref[t, :, lanes] = grad_probs
                totals.append(total[:, lanes] + fold(probs, jnp.sum))
                weights.append(weighted[:, lanes] + fold(probs * grad_probs, jnp.sum))
            return jnp.concatenate(totals, axis=1), jnp.concatenate(weights, axis=1)

        zeros = jnp.zeros((8, wide), jnp.float32)
        total, weighted = lax.fori_loop(0, tiles, probs_tile, (zeros, zeros))
        total = jnp.sum(total, axis=0, keepdims=True)
        logsum = top + jnp.log2(total)
        row_delta = jnp.sum(weighted, axis=0, keepdims=True) / total

        def backward_tile(t, carry):
            stored = place_ref[low_block + t]
            key_rows = pl.ds(pl.multiple_of(stored % 2 * block, block), block)
            key_tile = tile_of(t, 0)
            softmax = jnp.exp2(s_ref[t] - logsum)
            grad_scores = (softmax * (dp_ref[t] - row_delta)).astype(jnp.bfloat16)
            acc_ref[stored // 2, 1, key_rows, :] += dot_nn(
                softmax.astype(jnp.bfloat16), gs_ref[...]
            )
            acc_ref[stored // 2, 0, key_rows, :] += dot_nn(grad_scores, qs_ref[...])
            dqt_ref[...] += dot_tn(key_tile, grad_scores)
            return carry

        lax.fori_loop(0, tiles, backward_tile, 0)
        for h in range(heads):
            dq_ref[owner, rows, h * head_width : (h + 1) * head_width] = (
                jnp.transpose(dqt_ref[:, h * block : (h + 1) * block]) * scale
            ).astype(jnp.bfloat16)
        return carry

    lax.fori_loop(0, 4, one_strip, 0)
    dkv_ref[:, 0] = (acc_ref[:, 0] * scale).astype(dkv_ref.dtype)
    dkv_ref[:, 1] = acc_ref[:, 1].astype(dkv_ref.dtype)


def attention_backward(doc_lengths, assignment, queries, out_grad, queries_other, out_grad_other, kv):
    rows, width = queries.shape
    length = kv.shape[0] * rows
    block = rows // 2
    head_width = kv.shape[3]
    wide = width // head_width // 2 * block
    most = length // 2
    tiles = most // block + 1
    vmem = pl.BlockSpec(memory_space=pltpu.VMEM)
    smem = pl.BlockSpec(memory_space=pltpu.SMEM)
    return pl.pallas_call(
        attention_kernel,
        out_shape=(
            jax.ShapeDtypeStruct((2, rows, width // 2), jnp.bfloat16),
            jax.ShapeDtypeStruct(kv.shape, jnp.bfloat16),
        ),
        in_specs=[smem, smem, vmem, vmem, vmem, vmem, vmem],
        out_specs=(vmem, vmem),
        scratch_shapes=[
            pltpu.VMEM((wide, head_width), jnp.bfloat16),
            pltpu.VMEM((wide, head_width), jnp.bfloat16),
            pltpu.VMEM((tiles, block, wide), jnp.float32),
            pltpu.VMEM((tiles, block, wide), jnp.float32),
            pltpu.VMEM((8, wide), jnp.float32),
            pltpu.VMEM((head_width, wide), jnp.float32),
            pltpu.VMEM(kv.shape, jnp.float32),
            pltpu.SMEM((2 * assignment.shape[1],), jnp.int32),
        ],
        compiler_params=pltpu.CompilerParams(vmem_limit_bytes=60 * 1024 * 1024),
        name="attention_backward",
    )(doc_lengths, assignment, queries, out_grad, queries_other, out_grad_other, kv)


def local(queries, keys, values, out_grad, doc_lengths, assignment):
    kv, queries_other, out_grad_other = gather(keys[0], values[0], queries[0], out_grad[0])
    dq, dkv = attention_backward(
        doc_lengths, assignment, queries[0], out_grad[0], queries_other, out_grad_other, kv
    )
    query_in, key_in, value_in = reduce_and_pass(dq, dkv)
    return query_in[None], key_in[None], value_in[None]


def solution(mesh):
    return jax.shard_map(
        local,
        mesh=mesh,
        in_specs=(
            P("pipe", "ctx", None),
            P("pipe", "ctx", None),
            P("pipe", "ctx", None),
            P("pipe", "ctx", None),
            P("pipe", None),
            P("pipe", None),
        ),
        out_specs=(P("pipe", "ctx", None), P("pipe", "ctx", None), P("pipe", "ctx", None)),
        check_vma=False,
    )
```

```python
import functools
import math

import jax
import jax.numpy as jnp
from jax import lax
from jax.experimental import pallas as pl
from jax.experimental.pallas import tpu as pltpu
from jax.sharding import PartitionSpec as P

masked_score = -1e30


def dot_nt(a, b):
    return lax.dot_general(a, b, (((1,), (1,)), ((), ())), preferred_element_type=jnp.float32)


def dot_nn(a, b):
    return lax.dot_general(a, b, (((1,), (0,)), ((), ())), preferred_element_type=jnp.float32)


def dot_tn(a, b):
    return lax.dot_general(a, b, (((0,), (0,)), ((), ())), preferred_element_type=jnp.float32)


def chip_device(chip, core):
    return {"ctx": 2 * chip + core}


def greet(devices):
    barrier = pltpu.get_barrier_semaphore()
    for there, device in devices:

        @pl.when(there)
        def _():
            pl.semaphore_signal(
                barrier, inc=1, device_id=device, device_id_type=pl.DeviceIdType.MESH
            )

    count = sum(there.astype(jnp.int32) for there, device in devices)
    pl.semaphore_wait(barrier, count)


def remote(source, target, send_sem, recv_sem, device):
    return pltpu.make_async_remote_copy(
        src_ref=source,
        dst_ref=target,
        send_sem=send_sem,
        recv_sem=recv_sem,
        device_id=device,
        device_id_type=pl.DeviceIdType.MESH,
    )


def gather_kernel(
    k_ref,
    v_ref,
    q_ref,
    g_ref,
    kv_ref,
    qo_ref,
    go_ref,
    own_sem,
    line_send,
    line_recv,
    twin_send,
    twin_recv,
    swap_send,
    swap_recv,
):
    me = lax.axis_index("ctx")
    chips = kv_ref.shape[0] // 2
    half = qo_ref.shape[1]
    chip, core = me // 2, me % 2
    twin = chip_device(chip, 1 - core)
    has = (chip < chips - 1, chip > 0)
    ahead = (chip_device(chip + 1, core), chip_device(chip - 1, core))
    always = chip >= 0
    greet([(always, twin), (has[0], ahead[0]), (has[1], ahead[1])])

    sources = (k_ref, v_ref)
    own = [
        pltpu.make_async_copy(ref, kv_ref.at[me, part], own_sem.at[part])
        for part, ref in enumerate(sources)
    ]

    def shard_at(way, step):
        return 2 * (chip - step if way == 0 else chip + step) + core

    def along(way, step, hop, part):
        place = kv_ref.at[shard_at(way, step), part]
        return remote(
            sources[part] if hop == 0 and step == 0 else place,
            place,
            line_send.at[way, hop, part],
            line_recv.at[way, hop, part],
            ahead[way],
        )

    def across(way, step, part):
        place = kv_ref.at[shard_at(way, step), part]
        return remote(
            sources[part] if step == 0 else place,
            place,
            twin_send.at[way, step, part],
            twin_recv.at[way, step, part],
            twin,
        )

    def arriving(way, step):
        return chip - step >= 0 if way == 0 else chip + step < chips

    for part in range(2):
        for way in range(2):

            @pl.when(has[way])
            def _():
                along(way, 0, 0, part).start()

    for part in range(2):
        across(0, 0, part).start()
        own[part].start()
    lanes = pl.ds(pl.multiple_of((1 - core) * half, half), half)
    swaps = [
        remote(q_ref.at[:, lanes], qo_ref, swap_send.at[0], swap_recv.at[0], twin),
        remote(g_ref.at[:, lanes], go_ref, swap_send.at[1], swap_recv.at[1], twin),
    ]
    for copy in swaps:
        copy.start()
    for step in range(1, chips):
        for part in range(2):
            for way in range(2):

                @pl.when(arriving(way, step))
                def _():
                    along(way, step, step - 1, part).wait_recv()

                    @pl.when(has[way])
                    def _():
                        along(way, step, step, part).start()

                    across(way, step, part).start()

    for copy in swaps:
        copy.wait()
    for part in range(2):
        own[part].wait()
        across(0, 0, part).wait()
        for way in range(2):

            @pl.when(has[way])
            def _():
                along(way, 0, 0, part).wait_send()

    for step in range(1, chips):
        for part in range(2):
            for way in range(2):

                @pl.when(arriving(way, step))
                def _():
                    across(way, step, part).wait()

                    @pl.when(has[way])
                    def _():
                        along(way, step, step, part).wait_send()


def gather(keys, values, queries, out_grad):
    rows, width = queries.shape
    n_ctx = lax.axis_size("ctx")
    chips = n_ctx // 2
    half = width // 2
    return pl.pallas_call(
        gather_kernel,
        out_shape=(
            jax.ShapeDtypeStruct((n_ctx, 2) + keys.shape, keys.dtype),
            jax.ShapeDtypeStruct((rows, half), queries.dtype),
            jax.ShapeDtypeStruct((rows, half), queries.dtype),
        ),
        in_specs=[pl.BlockSpec(memory_space=pl.ANY)] * 4,
        out_specs=(pl.BlockSpec(memory_space=pl.ANY),) * 3,
        scratch_shapes=[
            pltpu.SemaphoreType.DMA((2,)),
            pltpu.SemaphoreType.DMA((2, chips, 2)),
            pltpu.SemaphoreType.DMA((2, chips, 2)),
            pltpu.SemaphoreType.DMA((2, chips, 2)),
            pltpu.SemaphoreType.DMA((2, chips, 2)),
            pltpu.SemaphoreType.DMA((2,)),
            pltpu.SemaphoreType.DMA((2,)),
        ],
        compiler_params=pltpu.CompilerParams(collective_id=0, has_side_effects=True),
        name="gather_blocks",
    )(keys, values, queries, out_grad)


def reduce_kernel(
    dq_own_ref,
    dq_other_ref,
    dkv_ref,
    late_ref,
    q_in_ref,
    k_in_ref,
    v_in_ref,
    mine_ref,
    twin_ref,
    line_ref,
    sum_ref,
    twin_send,
    twin_recv,
    line_send,
    line_recv,
    query_send,
    query_recv,
    last_send,
    last_recv,
    late_send,
    late_recv,
    mine_sem,
):
    me = lax.axis_index("ctx")
    stage = lax.axis_index("pipe")
    stages = lax.axis_size("pipe")
    chips = dkv_ref.shape[0] // 2
    block, half = dq_own_ref.shape
    chip, core = me // 2, me % 2
    twin = chip_device(chip, 1 - core)
    has = (chip < chips - 1, chip > 0)
    ahead = (chip_device(chip + 1, core), chip_device(chip - 1, core))
    always = chip >= 0
    before = lax.rem(stage + stages - 1, stages)
    after = lax.rem(stage + 1, stages)

    def own_part(z):
        return pltpu.make_async_copy(dkv_ref.at[2 * z + core], mine_ref.at[z], mine_sem.at[z])

    order = []
    for z in range(chips // 2):
        order += [z, chips - 1 - z]
    for z in order:
        own_part(z).start()
    greet(
        [(always, twin), (has[0], ahead[0]), (has[1], ahead[1])]
        + [
            (always, {"pipe": other, "ctx": 2 * chip + k})
            for other in (before, after)
            for k in range(2)
        ]
    )

    def crossing(z):
        return remote(
            dkv_ref.at[2 * z + 1 - core], twin_ref.at[z], twin_send.at[z], twin_recv.at[z], twin
        )

    for z in order:
        crossing(z).start()

    lanes = pl.ds(pl.multiple_of(core * half, half), half)

    ready = [
        remote(
            source,
            q_in_ref.at[:, lanes],
            query_send.at[index],
            query_recv.at[index],
            {"pipe": before, "ctx": 2 * chip + receiver},
        )
        for index, (source, receiver) in enumerate(
            ((dq_own_ref, core), (dq_other_ref, 1 - core))
        )
    ] + [
        remote(
            late_ref.at[pl.ds(part * block, block), :],
            ref.at[pl.ds(block, block), :],
            late_send.at[part],
            late_recv.at[part],
            {"pipe": before, "ctx": me},
        )
        for part, ref in enumerate((k_in_ref, v_in_ref))
    ]
    for copy in ready:
        copy.start()

    def passing(way, z, part):
        return remote(
            sum_ref.at[z, part],
            line_ref.at[way, z, part],
            line_send.at[way, z, part],
            line_recv.at[way, z, part],
            ahead[way],
        )

    def add_up(z, part, ways):
        total = mine_ref[z, part].astype(jnp.float32) + twin_ref[z, part].astype(
            jnp.float32
        )
        for way in ways:
            total += line_ref[way, z, part].astype(jnp.float32)
        sum_ref[z, part] = total.astype(sum_ref.dtype)

    for t in range(chips - 1):
        for part in range(2):
            for way in range(2):
                z = chips - 1 - (t - chip) if way == 0 else t - (chips - 1 - chip)
                beyond = (z <= chips - 1) & (z > chip) if way == 0 else (z >= 0) & (z < chip)

                @pl.when(beyond)
                def _():
                    if part == 0:
                        own_part(z).wait()
                        crossing(z).wait_recv()

                    @pl.when(has[1 - way])
                    def _():
                        passing(way, z, part).wait_recv()
                        add_up(z, part, (way,))

                    @pl.when(jnp.logical_not(has[1 - way]))
                    def _():
                        add_up(z, part, ())

                    passing(way, z, part).start()

    own_part(chip).wait()
    crossing(chip).wait_recv()
    lasts = []
    for part, ref in enumerate((k_in_ref, v_in_ref)):

        @pl.when(has[0] & has[1])
        def _():
            for way in range(2):
                passing(way, chip, part).wait_recv()
            add_up(chip, part, (0, 1))

        for way in range(2):

            @pl.when(jnp.logical_not(has[way]))
            def _():
                passing(way, chip, part).wait_recv()
                add_up(chip, part, (way,))

        lasts.append(
            remote(
                sum_ref.at[chip, part],
                ref.at[pl.ds(0, block), :],
                last_send.at[part],
                last_recv.at[part],
                {"pipe": before, "ctx": me},
            )
        )
        lasts[-1].start()
    for copy in ready:
        copy.wait()
    for z in range(chips):
        crossing(z).wait_send()
        for part in range(2):

            @pl.when(z > chip)
            def _():
                passing(0, z, part).wait_send()

            @pl.when(z < chip)
            def _():
                passing(1, z, part).wait_send()

    for copy in lasts:
        copy.wait()


def reduce_and_pass(dq_own, dq_other, dkv, late):
    block, half = dq_own.shape
    n_ctx, _, _, head_width = dkv.shape
    chips = n_ctx // 2
    part = dkv.shape[1:]
    return pl.pallas_call(
        reduce_kernel,
        out_shape=(
            jax.ShapeDtypeStruct((block, 2 * half), dkv.dtype),
            jax.ShapeDtypeStruct((2 * block, head_width), dkv.dtype),
            jax.ShapeDtypeStruct((2 * block, head_width), dkv.dtype),
        ),
        in_specs=[pl.BlockSpec(memory_space=pl.ANY)] * 4,
        out_specs=(pl.BlockSpec(memory_space=pl.ANY),) * 3,
        scratch_shapes=[
            pltpu.VMEM((chips,) + part, dkv.dtype),
            pltpu.VMEM((chips,) + part, dkv.dtype),
            pltpu.VMEM((2, chips) + part, dkv.dtype),
            pltpu.VMEM((chips,) + part, dkv.dtype),
            pltpu.SemaphoreType.DMA((chips,)),
            pltpu.SemaphoreType.DMA((chips,)),
            pltpu.SemaphoreType.DMA((2, chips, 2)),
            pltpu.SemaphoreType.DMA((2, chips, 2)),
            pltpu.SemaphoreType.DMA((2,)),
            pltpu.SemaphoreType.DMA((2,)),
            pltpu.SemaphoreType.DMA((2,)),
            pltpu.SemaphoreType.DMA((2,)),
            pltpu.SemaphoreType.DMA((2,)),
            pltpu.SemaphoreType.DMA((2,)),
            pltpu.SemaphoreType.DMA((chips,)),
        ],
        compiler_params=pltpu.CompilerParams(
            collective_id=1, has_side_effects=True, vmem_limit_bytes=60 * 1024 * 1024
        ),
        name="reduce_and_pass",
    )(dq_own, dq_other, dkv, late)


def attention_kernel(
    slot,
    sizes_ref,
    placing_ref,
    q_ref,
    g_ref,
    qo_ref,
    go_ref,
    kv_ref,
    *rest,
):
    if slot == 0:
        low_ref, dq_own_ref, dq_other_ref, dkv_ref = rest[:4]
    else:
        dq_own_ref, dq_other_ref, dkv_ref, low_ref = rest[:4]
    qs_ref, gs_ref, s_ref, dp_ref, top_ref, dqt_ref, acc_ref, place_ref = rest[4:]
    block = q_ref.shape[0]
    head_width = kv_ref.shape[3]
    head_count = q_ref.shape[1] // head_width
    n_ctx = placing_ref.shape[1]
    n_docs = sizes_ref.shape[1]
    heads = head_count // 2
    wide = heads * block
    scale = 1.0 / math.sqrt(head_width)
    scale2 = scale * math.log2(math.e)
    me = lax.axis_index("ctx")
    chip, core = me // 2, me % 2

    starts = [jnp.int32(0)]
    for d in range(n_docs - 1):
        starts.append(starts[-1] + sizes_ref[0, d])
    for d in range(n_ctx):
        low = placing_ref[0, d]
        place_ref[low] = 2 * d
        place_ref[2 * n_ctx - 1 - low] = 2 * d + 1
    if slot == 0:
        acc_ref[0] = low_ref[...]
    else:
        acc_ref[...] = jnp.zeros_like(acc_ref)

    def one_strip(owner, carry):
        placed = placing_ref[0, 2 * chip + owner]
        query_block = placed if slot == 0 else 2 * n_ctx - 1 - placed

        @pl.when(owner == core)
        def _():
            for h in range(heads):
                lanes = pl.ds(
                    pl.multiple_of((core * heads + h) * head_width, head_width), head_width
                )
                qs_ref[h * block : (h + 1) * block, :] = q_ref[:, lanes]
                gs_ref[h * block : (h + 1) * block, :] = g_ref[:, lanes]

        @pl.when(owner != core)
        def _():
            for h in range(heads):
                lanes = slice(h * head_width, (h + 1) * head_width)
                qs_ref[h * block : (h + 1) * block, :] = qo_ref[:, lanes]
                gs_ref[h * block : (h + 1) * block, :] = go_ref[:, lanes]

        first = query_block * block
        query_pos = first + lax.broadcasted_iota(jnp.int32, (1, block), 1)
        doc_first = jnp.zeros((1, block), jnp.int32)
        strip_first = jnp.int32(0)
        for start in starts[1:]:
            doc_first = jnp.where(query_pos >= start, start, doc_first)
            strip_first = jnp.where(first >= start, start, strip_first)
        low_block = strip_first // block
        tiles = query_block - low_block + 1
        dqt_ref[...] = jnp.zeros_like(dqt_ref)

        last_doc = jnp.int32(0)
        for start in starts[1:]:
            last_doc = jnp.where(first + block - 1 >= start, start, last_doc)
        top_ref[...] = jnp.full(top_ref.shape, masked_score, jnp.float32)

        def tile_of(t, part):
            stored = place_ref[low_block + t]
            key_rows = pl.ds(pl.multiple_of(stored % 2 * block, block), block)
            return kv_ref[stored // 2, part, key_rows, :]

        def fold(x, combine):
            return combine(x.reshape(block // 8, 8, block), axis=0)

        def score_tile(t, carry):
            key_first = (low_block + t) * block
            key_tile = tile_of(t, 0)
            partial = (t == tiles - 1) | (key_first < last_doc)

            def scores_of(allowed):
                for h in range(heads):
                    lanes = slice(h * block, (h + 1) * block)
                    scores = dot_nt(key_tile, qs_ref[lanes, :]) * scale2
                    if allowed is not None:
                        scores = jnp.where(allowed, scores, masked_score)
                    s_ref[t, :, lanes] = scores
                    top_ref[:, lanes] = jnp.maximum(top_ref[:, lanes], fold(scores, jnp.max))

            @pl.when(partial)
            def _():
                key_pos = key_first + lax.broadcasted_iota(jnp.int32, (block, block), 0)
                scores_of((key_pos <= query_pos) & (key_pos >= doc_first))

            @pl.when(jnp.logical_not(partial))
            def _():
                scores_of(None)

            return carry

        lax.fori_loop(0, tiles, score_tile, 0)
        top = jnp.max(top_ref[...], axis=0, keepdims=True)

        def probs_tile(t, state):
            total, weighted = state
            value_tile = tile_of(t, 1)
            totals, weights = [], []
            for h in range(heads):
                lanes = slice(h * block, (h + 1) * block)
                grad_probs = dot_nt(value_tile, gs_ref[lanes, :])
                probs = jnp.exp2(s_ref[t, :, lanes] - top[:, lanes])
                dp_ref[t, :, lanes] = grad_probs
                totals.append(total[:, lanes] + fold(probs, jnp.sum))
                weights.append(weighted[:, lanes] + fold(probs * grad_probs, jnp.sum))
            return jnp.concatenate(totals, axis=1), jnp.concatenate(weights, axis=1)

        zeros = jnp.zeros((8, wide), jnp.float32)
        total, weighted = lax.fori_loop(0, tiles, probs_tile, (zeros, zeros))
        total = jnp.sum(total, axis=0, keepdims=True)
        logsum = top + jnp.log2(total)
        row_delta = jnp.sum(weighted, axis=0, keepdims=True) / total

        def backward_tile(t, carry):
            stored = place_ref[low_block + t]
            key_tile = tile_of(t, 0)
            softmax = jnp.exp2(s_ref[t] - logsum)
            grad_scores = (softmax * (dp_ref[t] - row_delta)).astype(jnp.bfloat16)
            acc_ref[stored % 2, stored // 2, 1] += dot_nn(
                softmax.astype(jnp.bfloat16), gs_ref[...]
            )
            acc_ref[stored % 2, stored // 2, 0] += dot_nn(grad_scores, qs_ref[...])
            dqt_ref[...] += dot_tn(key_tile, grad_scores)
            return carry

        lax.fori_loop(0, tiles, backward_tile, 0)
        def store_grad(dq_ref):
            for h in range(heads):
                dq_ref[:, h * head_width : (h + 1) * head_width] = (
                    jnp.transpose(dqt_ref[:, h * block : (h + 1) * block]) * scale
                ).astype(jnp.bfloat16)

        @pl.when(owner == core)
        def _():
            store_grad(dq_own_ref)

        @pl.when(owner != core)
        def _():
            store_grad(dq_other_ref)

        return carry

    lax.fori_loop(0, 2, one_strip, 0)
    dkv_ref[:, 0] = (acc_ref[slot, :, 0] * scale).astype(dkv_ref.dtype)
    dkv_ref[:, 1] = acc_ref[slot, :, 1].astype(dkv_ref.dtype)
    if slot == 1:
        low_ref[...] = acc_ref[0]


def attention_backward(
    slot, doc_lengths, assignment, queries, out_grad, queries_other, out_grad_other, kv, *low
):
    rows, width = queries.shape
    n_ctx, _, _, head_width = kv.shape
    block = rows // 2
    wide = width // head_width // 2 * block
    most = n_ctx * rows // 2
    tiles = most // block + 1
    vmem = pl.BlockSpec(memory_space=pltpu.VMEM)
    smem = pl.BlockSpec(memory_space=pltpu.SMEM)
    once = pl.Buffered(1)
    own_rows = pl.BlockSpec((block, width), lambda i: (slot, 0), pipeline_mode=once)
    other_rows = pl.BlockSpec((block, width // 2), lambda i: (slot, 0), pipeline_mode=once)
    keys_to = pl.BlockSpec(
        (n_ctx, 2, block * (1 + slot), head_width), lambda i: (0, 0, 0, 0), pipeline_mode=once
    )
    grads = jax.ShapeDtypeStruct((block, width // 2), jnp.bfloat16)
    kv_half = (n_ctx, 2, block, head_width)
    out_shape = [grads, grads, jax.ShapeDtypeStruct(kv_half, jnp.bfloat16)]
    if slot == 1:
        out_shape.append(jax.ShapeDtypeStruct(kv_half, jnp.float32))
    return pl.pallas_call(
        functools.partial(attention_kernel, slot),
        out_shape=out_shape,
        in_specs=[smem, smem, own_rows, own_rows, other_rows, other_rows, keys_to]
        + [vmem] * len(low),
        out_specs=[vmem] * len(out_shape),
        grid=(1,),
        scratch_shapes=[
            pltpu.VMEM((wide, head_width), jnp.bfloat16),
            pltpu.VMEM((wide, head_width), jnp.bfloat16),
            pltpu.VMEM((tiles, block, wide), jnp.float32),
            pltpu.VMEM((tiles, block, wide), jnp.float32),
            pltpu.VMEM((8, wide), jnp.float32),
            pltpu.VMEM((head_width, wide), jnp.float32),
            pltpu.VMEM((1 + slot,) + kv_half, jnp.float32),
            pltpu.SMEM((2 * n_ctx,), jnp.int32),
        ],
        compiler_params=pltpu.CompilerParams(vmem_limit_bytes=60 * 1024 * 1024),
        cost_estimate=pl.CostEstimate(
            flops=10 * 10**9, bytes_accessed=6 * 10**6, transcendentals=5 * 10**6
        ),
        name="attention_late_half" if slot else "attention_early_half",
    )(doc_lengths, assignment, queries, out_grad, queries_other, out_grad_other, kv, *low)


def local(queries, keys, values, out_grad, doc_lengths, assignment):
    kv, queries_other, out_grad_other = gather(keys[0], values[0], queries[0], out_grad[0])
    taken = (doc_lengths, assignment, queries[0], out_grad[0], queries_other, out_grad_other, kv)
    late_own, late_other, late_dkv, low = attention_backward(1, *taken)
    stages, n_ctx = lax.axis_size("pipe"), lax.axis_size("ctx")
    late_sum = lax.psum_scatter(
        late_dkv.reshape(-1, late_dkv.shape[-1]), "ctx", scatter_dimension=0, tiled=True
    )
    route_own, route_other = [], []
    for stage in range(stages):
        before = (stage + stages - 1) % stages
        for i in range(n_ctx):
            route_own.append((stage * n_ctx + i, before * n_ctx + i))
            route_other.append((stage * n_ctx + i, before * n_ctx + i // 2 * 2 + 1 - i % 2))
    late_own = lax.ppermute(late_own, ("pipe", "ctx"), route_own)
    late_other = lax.ppermute(late_other, ("pipe", "ctx"), route_other)
    early_own, early_other, dkv = attention_backward(0, *taken, low)
    early, key_in, value_in = reduce_and_pass(early_own, early_other, dkv, late_sum)
    first_core = lax.axis_index("ctx") % 2 == 0
    late = jnp.concatenate(
        [
            jnp.where(first_core, late_own, late_other),
            jnp.where(first_core, late_other, late_own),
        ],
        axis=1,
    )
    query_in = jnp.concatenate([early, late], axis=0)
    return query_in[None], key_in[None], value_in[None]


def solution(mesh):
    return jax.shard_map(
        local,
        mesh=mesh,
        in_specs=(
            P("pipe", "ctx", None),
            P("pipe", "ctx", None),
            P("pipe", "ctx", None),
            P("pipe", "ctx", None),
            P("pipe", None),
            P("pipe", None),
        ),
        out_specs=(P("pipe", "ctx", None), P("pipe", "ctx", None), P("pipe", "ctx", None)),
        check_vma=False,
    )
```

```python
import math

import jax
import jax.numpy as jnp
from jax import lax
from jax.experimental import pallas as pl
from jax.experimental.pallas import tpu as pltpu
from jax.sharding import PartitionSpec as P

masked_score = -1e30


def dot_nt(a, b):
    return lax.dot_general(a, b, (((1,), (1,)), ((), ())), preferred_element_type=jnp.float32)


def dot_nn(a, b):
    return lax.dot_general(a, b, (((1,), (0,)), ((), ())), preferred_element_type=jnp.float32)


def dot_tn(a, b):
    return lax.dot_general(a, b, (((0,), (0,)), ((), ())), preferred_element_type=jnp.float32)


def chip_device(chip, core):
    return {"ctx": 2 * chip + core}


def greet(devices):
    barrier = pltpu.get_barrier_semaphore()
    for there, device in devices:

        @pl.when(there)
        def _():
            pl.semaphore_signal(
                barrier, inc=1, device_id=device, device_id_type=pl.DeviceIdType.MESH
            )

    count = sum(there.astype(jnp.int32) for there, device in devices)
    pl.semaphore_wait(barrier, count)


def remote(source, target, send_sem, recv_sem, device):
    return pltpu.make_async_remote_copy(
        src_ref=source,
        dst_ref=target,
        send_sem=send_sem,
        recv_sem=recv_sem,
        device_id=device,
        device_id_type=pl.DeviceIdType.MESH,
    )


def gather_kernel(
    k_ref,
    v_ref,
    q_ref,
    g_ref,
    kv_ref,
    qo_ref,
    go_ref,
    own_sem,
    line_send,
    line_recv,
    twin_send,
    twin_recv,
    swap_send,
    swap_recv,
):
    me = lax.axis_index("ctx")
    chips = kv_ref.shape[0] // 2
    half = qo_ref.shape[1]
    chip, core = me // 2, me % 2
    twin = chip_device(chip, 1 - core)
    has = (chip < chips - 1, chip > 0)
    ahead = (chip_device(chip + 1, core), chip_device(chip - 1, core))
    always = chip >= 0
    greet([(always, twin), (has[0], ahead[0]), (has[1], ahead[1])])

    sources = (k_ref, v_ref)
    own = [
        pltpu.make_async_copy(ref, kv_ref.at[me, part], own_sem.at[part])
        for part, ref in enumerate(sources)
    ]

    def shard_at(way, step):
        return 2 * (chip - step if way == 0 else chip + step) + core

    def along(way, step, hop, part):
        place = kv_ref.at[shard_at(way, step), part]
        return remote(
            sources[part] if hop == 0 and step == 0 else place,
            place,
            line_send.at[way, hop, part],
            line_recv.at[way, hop, part],
            ahead[way],
        )

    def across(way, step, part):
        place = kv_ref.at[shard_at(way, step), part]
        return remote(
            sources[part] if step == 0 else place,
            place,
            twin_send.at[way, step, part],
            twin_recv.at[way, step, part],
            twin,
        )

    def arriving(way, step):
        return chip - step >= 0 if way == 0 else chip + step < chips

    for part in range(2):
        for way in range(2):

            @pl.when(has[way])
            def _():
                along(way, 0, 0, part).start()

    for part in range(2):
        across(0, 0, part).start()
        own[part].start()
    lanes = pl.ds(pl.multiple_of((1 - core) * half, half), half)
    swaps = [
        remote(q_ref.at[:, lanes], qo_ref, swap_send.at[0], swap_recv.at[0], twin),
        remote(g_ref.at[:, lanes], go_ref, swap_send.at[1], swap_recv.at[1], twin),
    ]
    for copy in swaps:
        copy.start()
    for step in range(1, chips):
        for part in range(2):
            for way in range(2):

                @pl.when(arriving(way, step))
                def _():
                    along(way, step, step - 1, part).wait_recv()

                    @pl.when(has[way])
                    def _():
                        along(way, step, step, part).start()

                    across(way, step, part).start()

    for copy in swaps:
        copy.wait()
    for part in range(2):
        own[part].wait()
        across(0, 0, part).wait()
        for way in range(2):

            @pl.when(has[way])
            def _():
                along(way, 0, 0, part).wait_send()

    for step in range(1, chips):
        for part in range(2):
            for way in range(2):

                @pl.when(arriving(way, step))
                def _():
                    across(way, step, part).wait()

                    @pl.when(has[way])
                    def _():
                        along(way, step, step, part).wait_send()


def gather(keys, values, queries, out_grad):
    rows, width = queries.shape
    n_ctx = lax.axis_size("ctx")
    chips = n_ctx // 2
    half = width // 2
    return pl.pallas_call(
        gather_kernel,
        out_shape=(
            jax.ShapeDtypeStruct((n_ctx, 2) + keys.shape, keys.dtype),
            jax.ShapeDtypeStruct((rows, half), queries.dtype),
            jax.ShapeDtypeStruct((rows, half), queries.dtype),
        ),
        in_specs=[pl.BlockSpec(memory_space=pl.ANY)] * 4,
        out_specs=(pl.BlockSpec(memory_space=pl.ANY),) * 3,
        scratch_shapes=[
            pltpu.SemaphoreType.DMA((2,)),
            pltpu.SemaphoreType.DMA((2, chips, 2)),
            pltpu.SemaphoreType.DMA((2, chips, 2)),
            pltpu.SemaphoreType.DMA((2, chips, 2)),
            pltpu.SemaphoreType.DMA((2, chips, 2)),
            pltpu.SemaphoreType.DMA((2,)),
            pltpu.SemaphoreType.DMA((2,)),
        ],
        compiler_params=pltpu.CompilerParams(collective_id=0, has_side_effects=True),
        name="gather_blocks",
    )(keys, values, queries, out_grad)


def reduce_kernel(
    dq_ref,
    dkv_ref,
    q_in_ref,
    kv_in_ref,
    mine_ref,
    twin_ref,
    line_ref,
    sum_ref,
    twin_send,
    twin_recv,
    line_send,
    line_recv,
    query_send,
    query_recv,
    last_send,
    last_recv,
    mine_sem,
):
    me = lax.axis_index("ctx")
    stage = lax.axis_index("pipe")
    stages = lax.axis_size("pipe")
    chips = dkv_ref.shape[0] // 2
    half = dq_ref.shape[2]
    chip, core = me // 2, me % 2
    twin = chip_device(chip, 1 - core)
    has = (chip < chips - 1, chip > 0)
    ahead = (chip_device(chip + 1, core), chip_device(chip - 1, core))
    always = chip >= 0
    before = lax.rem(stage + stages - 1, stages)
    after = lax.rem(stage + 1, stages)

    def own_part(z):
        return pltpu.make_async_copy(dkv_ref.at[2 * z + core], mine_ref.at[z], mine_sem.at[z])

    order = []
    for z in range(chips // 2):
        order += [z, chips - 1 - z]
    for z in order:
        own_part(z).start()
    greet(
        [(always, twin), (has[0], ahead[0]), (has[1], ahead[1])]
        + [
            (always, {"pipe": other, "ctx": 2 * chip + k})
            for other in (before, after)
            for k in range(2)
        ]
    )

    def crossing(z):
        return remote(
            dkv_ref.at[2 * z + 1 - core], twin_ref.at[z], twin_send.at[z], twin_recv.at[z], twin
        )

    for z in order:
        crossing(z).start()

    lanes = pl.ds(pl.multiple_of(core * half, half), half)

    def query_copy(k, recv_index):
        return remote(
            dq_ref.at[k],
            q_in_ref.at[:, lanes],
            query_send.at[k],
            query_recv.at[recv_index],
            {"pipe": before, "ctx": 2 * chip + k},
        )

    for k in range(2):
        query_copy(k, core).start()

    def passing(way, z, part):
        return remote(
            sum_ref.at[z, part],
            line_ref.at[way, z, part],
            line_send.at[way, z, part],
            line_recv.at[way, z, part],
            ahead[way],
        )

    def add_up(z, part, ways):
        total = mine_ref[z, part].astype(jnp.float32) + twin_ref[z, part].astype(
            jnp.float32
        )
        for way in ways:
            total += line_ref[way, z, part].astype(jnp.float32)
        sum_ref[z, part] = total.astype(sum_ref.dtype)

    for t in range(chips - 1):
        for part in range(2):
            for way in range(2):
                z = chips - 1 - (t - chip) if way == 0 else t - (chips - 1 - chip)
                beyond = (z <= chips - 1) & (z > chip) if way == 0 else (z >= 0) & (z < chip)

                @pl.when(beyond)
                def _():
                    if part == 0:
                        own_part(z).wait()
                        crossing(z).wait_recv()

                    @pl.when(has[1 - way])
                    def _():
                        passing(way, z, part).wait_recv()
                        add_up(z, part, (way,))

                    @pl.when(jnp.logical_not(has[1 - way]))
                    def _():
                        add_up(z, part, ())

                    passing(way, z, part).start()

    own_part(chip).wait()
    crossing(chip).wait_recv()
    lasts = []
    for part in range(2):

        @pl.when(has[0] & has[1])
        def _():
            for way in range(2):
                passing(way, chip, part).wait_recv()
            add_up(chip, part, (0, 1))

        for way in range(2):

            @pl.when(jnp.logical_not(has[way]))
            def _():
                passing(way, chip, part).wait_recv()
                add_up(chip, part, (way,))

        lasts.append(
            remote(
                sum_ref.at[chip, part],
                kv_in_ref.at[part],
                last_send.at[part],
                last_recv.at[part],
                {"pipe": before, "ctx": me},
            )
        )
        lasts[-1].start()
    for k in range(2):
        query_copy(k, k).wait()
    for z in range(chips):
        crossing(z).wait_send()
        for part in range(2):

            @pl.when(z > chip)
            def _():
                passing(0, z, part).wait_send()

            @pl.when(z < chip)
            def _():
                passing(1, z, part).wait_send()

    for copy in lasts:
        copy.wait()


def reduce_and_pass(dq, dkv):
    rows, half = dq.shape[1:]
    n_ctx, _, _, head_width = dkv.shape
    chips = n_ctx // 2
    part = dkv.shape[1:]
    return pl.pallas_call(
        reduce_kernel,
        out_shape=(
            jax.ShapeDtypeStruct((rows, 2 * half), dq.dtype),
            jax.ShapeDtypeStruct((2, rows, head_width), dq.dtype),
        ),
        in_specs=[pl.BlockSpec(memory_space=pl.ANY)] * 2,
        out_specs=(pl.BlockSpec(memory_space=pl.ANY),) * 2,
        scratch_shapes=[
            pltpu.VMEM((chips,) + part, dkv.dtype),
            pltpu.VMEM((chips,) + part, dkv.dtype),
            pltpu.VMEM((2, chips) + part, dkv.dtype),
            pltpu.VMEM((chips,) + part, dkv.dtype),
            pltpu.SemaphoreType.DMA((chips,)),
            pltpu.SemaphoreType.DMA((chips,)),
            pltpu.SemaphoreType.DMA((2, chips, 2)),
            pltpu.SemaphoreType.DMA((2, chips, 2)),
            pltpu.SemaphoreType.DMA((2,)),
            pltpu.SemaphoreType.DMA((2,)),
            pltpu.SemaphoreType.DMA((2,)),
            pltpu.SemaphoreType.DMA((2,)),
            pltpu.SemaphoreType.DMA((chips,)),
        ],
        compiler_params=pltpu.CompilerParams(
            collective_id=1, has_side_effects=True, vmem_limit_bytes=16 * 1024 * 1024
        ),
        name="reduce_and_pass",
    )(dq, dkv)


def attention_kernel(
    sizes_ref,
    placing_ref,
    q_ref,
    g_ref,
    qo_ref,
    go_ref,
    kv_ref,
    dq_ref,
    dkv_ref,
    qs_ref,
    gs_ref,
    s_ref,
    dp_ref,
    top_ref,
    total_ref,
    weighted_ref,
    logsum_ref,
    delta_ref,
    *rest,
):
    low_refs = (rest[:2], rest[2:4])
    dqt_ref, acc_ref, place_ref = rest[4:]
    block = q_ref.shape[0] // 2
    head_width = kv_ref.shape[3]
    head_count = q_ref.shape[1] // head_width
    n_ctx = placing_ref.shape[1]
    n_docs = sizes_ref.shape[1]
    heads = head_count // 2
    wide = heads * block
    scale = 1.0 / math.sqrt(head_width)
    scale2 = scale * math.log2(math.e)
    me = lax.axis_index("ctx")
    chip, core = me // 2, me % 2

    starts = [jnp.int32(0)]
    for d in range(n_docs - 1):
        starts.append(starts[-1] + sizes_ref[0, d])
    for d in range(n_ctx):
        low = placing_ref[0, d]
        place_ref[low] = 2 * d
        place_ref[2 * n_ctx - 1 - low] = 2 * d + 1
    acc_ref[...] = jnp.zeros_like(acc_ref)

    def one_strip(step, carry):
        owner = step // 2
        slot = step % 2
        placed = placing_ref[0, 2 * chip + owner]
        query_block = jnp.where(slot == 0, placed, 2 * n_ctx - 1 - placed)
        rows = pl.ds(pl.multiple_of(slot * block, block), block)

        @pl.when(owner == core)
        def _():
            for h in range(heads):
                lanes = pl.ds(
                    pl.multiple_of((core * heads + h) * head_width, head_width), head_width
                )
                qs_ref[h * block : (h + 1) * block, :] = q_ref[rows, lanes]
                gs_ref[h * block : (h + 1) * block, :] = g_ref[rows, lanes]

        @pl.when(owner != core)
        def _():
            for h in range(heads):
                lanes = slice(h * head_width, (h + 1) * head_width)
                qs_ref[h * block : (h + 1) * block, :] = qo_ref[rows, lanes]
                gs_ref[h * block : (h + 1) * block, :] = go_ref[rows, lanes]

        first = query_block * block
        query_pos = first + lax.broadcasted_iota(jnp.int32, (1, block), 1)
        doc_first = jnp.zeros((1, block), jnp.int32)
        strip_first = jnp.int32(0)
        for start in starts[1:]:
            doc_first = jnp.where(query_pos >= start, start, doc_first)
            strip_first = jnp.where(first >= start, start, strip_first)
        low_block = strip_first // block
        tiles = query_block - low_block + 1
        dqt_ref[...] = jnp.zeros_like(dqt_ref)

        last_doc = jnp.int32(0)
        for start in starts[1:]:
            last_doc = jnp.where(first + block - 1 >= start, start, last_doc)
        top_ref[...] = jnp.full(top_ref.shape, masked_score, jnp.float32)
        total_ref[...] = jnp.zeros_like(total_ref)
        weighted_ref[...] = jnp.zeros_like(weighted_ref)

        def tile_of(t, part):
            stored = place_ref[low_block + t]
            key_rows = pl.ds(pl.multiple_of(stored % 2 * block, block), block)
            return kv_ref[stored // 2, part, key_rows, :]

        def fold(x, combine):
            return combine(x.reshape(block // 8, 8, block), axis=0)

        def forward(tiles_now, masked):
            allowed, key_tiles, value_tiles = [], [], []
            for t in tiles_now:
                key_tiles.append(tile_of(t, 0))
                value_tiles.append(tile_of(t, 1))
                if masked:
                    key_pos = (low_block + t) * block + lax.broadcasted_iota(
                        jnp.int32, (block, block), 0
                    )
                    allowed.append((key_pos <= query_pos) & (key_pos >= doc_first))
            tops = []
            for h in range(heads):
                lanes = slice(h * block, (h + 1) * block)
                top = top_ref[:, lanes]
                for i, t in enumerate(tiles_now):
                    scores = dot_nt(key_tiles[i], qs_ref[lanes, :]) * scale2
                    if masked:
                        scores = jnp.where(allowed[i], scores, masked_score)
                    s_ref[t, :, lanes] = scores
                    top = jnp.maximum(top, jnp.max(fold(scores, jnp.max), axis=0, keepdims=True))
                tops.append(top)
            for h in range(heads):
                lanes = slice(h * block, (h + 1) * block)
                factor = jnp.exp2(top_ref[:, lanes] - tops[h])
                top_ref[:, lanes] = tops[h]
                total = total_ref[:, lanes] * factor
                weighted = weighted_ref[:, lanes] * factor
                for i, t in enumerate(tiles_now):
                    grad_probs = dot_nt(value_tiles[i], gs_ref[lanes, :])
                    dp_ref[t, :, lanes] = grad_probs
                    probs = jnp.exp2(s_ref[t, :, lanes] - tops[h])
                    total += fold(probs, jnp.sum)
                    weighted += fold(probs * grad_probs, jnp.sum)
                total_ref[:, lanes] = total
                weighted_ref[:, lanes] = weighted

        def forward_guarded(tiles_now):
            partial = tiles_now[-1] == tiles - 1
            partial |= (low_block + tiles_now[0]) * block < last_doc

            @pl.when(partial)
            def _():
                forward(tiles_now, True)

            @pl.when(jnp.logical_not(partial))
            def _():
                forward(tiles_now, False)

        def backward(tiles_now):
            for i, t in enumerate(tiles_now):
                stored = place_ref[low_block + t]
                key_rows = pl.ds(pl.multiple_of(stored % 2 * block, block), block)
                key_tile = tile_of(t, 0)
                for h in range(heads):
                    lanes = slice(h * block, (h + 1) * block)
                    for r in range(0, block, 64):
                        softmax = jnp.exp2(s_ref[t, r : r + 64, lanes] - logsum_ref[:, lanes])
                        grad_scores = softmax * (dp_ref[t, r : r + 64, lanes] - delta_ref[:, lanes])
                        low_refs[i][0][r : r + 64, lanes] = softmax.astype(jnp.bfloat16)
                        low_refs[i][1][r : r + 64, lanes] = grad_scores.astype(jnp.bfloat16)
                acc_ref[stored // 2, 1, key_rows, :] += dot_nn(low_refs[i][0][...], gs_ref[...])
                acc_ref[stored // 2, 0, key_rows, :] += dot_nn(low_refs[i][1][...], qs_ref[...])
                dqt_ref[...] += dot_tn(key_tile, low_refs[i][1][...])

        def over_tiles(work):
            def pair(i, carry):
                work([2 * i, 2 * i + 1])
                return carry

            lax.fori_loop(0, tiles // 2, pair, 0)

            @pl.when(tiles % 2 == 1)
            def _():
                work([tiles - 1])

        over_tiles(forward_guarded)
        total = jnp.sum(total_ref[...], axis=0, keepdims=True)
        logsum_ref[...] = top_ref[...] + jnp.log2(total)
        delta_ref[...] = jnp.sum(weighted_ref[...], axis=0, keepdims=True) / total
        over_tiles(backward)
        for h in range(heads):
            dq_ref[owner, rows, h * head_width : (h + 1) * head_width] = (
                jnp.transpose(dqt_ref[:, h * block : (h + 1) * block]) * scale
            ).astype(jnp.bfloat16)
        return carry

    lax.fori_loop(0, 4, one_strip, 0)
    dkv_ref[:, 0] = (acc_ref[:, 0] * scale).astype(dkv_ref.dtype)
    dkv_ref[:, 1] = acc_ref[:, 1].astype(dkv_ref.dtype)


def attention_backward(doc_lengths, assignment, queries, out_grad, queries_other, out_grad_other, kv):
    rows, width = queries.shape
    length = kv.shape[0] * rows
    block = rows // 2
    head_width = kv.shape[3]
    wide = width // head_width // 2 * block
    most = length // 2
    tiles = most // block + 1
    strips = 2 * tiles * block * wide * 4
    limit = strips + 4 * length * head_width * 4 + 20 * rows * width + 6 * 1024 * 1024
    vmem = pl.BlockSpec(memory_space=pltpu.VMEM)
    smem = pl.BlockSpec(memory_space=pltpu.SMEM)
    return pl.pallas_call(
        attention_kernel,
        out_shape=(
            jax.ShapeDtypeStruct((2, rows, width // 2), jnp.bfloat16),
            jax.ShapeDtypeStruct(kv.shape, jnp.bfloat16),
        ),
        in_specs=[smem, smem, vmem, vmem, vmem, vmem, vmem],
        out_specs=(vmem, vmem),
        scratch_shapes=[
            pltpu.VMEM((wide, head_width), jnp.bfloat16),
            pltpu.VMEM((wide, head_width), jnp.bfloat16),
            pltpu.VMEM((tiles, block, wide), jnp.float32),
            pltpu.VMEM((tiles, block, wide), jnp.float32),
            pltpu.VMEM((1, wide), jnp.float32),
            pltpu.VMEM((8, wide), jnp.float32),
            pltpu.VMEM((8, wide), jnp.float32),
            pltpu.VMEM((1, wide), jnp.float32),
            pltpu.VMEM((1, wide), jnp.float32),
            pltpu.VMEM((block, wide), jnp.bfloat16),
            pltpu.VMEM((block, wide), jnp.bfloat16),
            pltpu.VMEM((block, wide), jnp.bfloat16),
            pltpu.VMEM((block, wide), jnp.bfloat16),
            pltpu.VMEM((head_width, wide), jnp.float32),
            pltpu.VMEM(kv.shape, jnp.float32),
            pltpu.SMEM((2 * assignment.shape[1],), jnp.int32),
        ],
        compiler_params=pltpu.CompilerParams(vmem_limit_bytes=limit),
        name="attention_backward",
    )(doc_lengths, assignment, queries, out_grad, queries_other, out_grad_other, kv)


def local(queries, keys, values, out_grad, doc_lengths, assignment):
    kv, queries_other, out_grad_other = gather(keys[0], values[0], queries[0], out_grad[0])
    dq, dkv = attention_backward(
        doc_lengths, assignment, queries[0], out_grad[0], queries_other, out_grad_other, kv
    )
    query_in, kv_in = reduce_and_pass(dq, dkv)
    return query_in[None], kv_in[0][None], kv_in[1][None]


def solution(mesh):
    return jax.shard_map(
        local,
        mesh=mesh,
        in_specs=(
            P("pipe", "ctx", None),
            P("pipe", "ctx", None),
            P("pipe", "ctx", None),
            P("pipe", "ctx", None),
            P("pipe", None),
            P("pipe", None),
        ),
        out_specs=(P("pipe", "ctx", None), P("pipe", "ctx", None), P("pipe", "ctx", None)),
        check_vma=False,
    )
```

```python
import math

import jax
import jax.numpy as jnp
from jax import lax
from jax.experimental import pallas as pl
from jax.experimental.pallas import tpu as pltpu
from jax.sharding import PartitionSpec as P

masked_score = -1e30


def dot_nt(a, b):
    return lax.dot_general(a, b, (((1,), (1,)), ((), ())), preferred_element_type=jnp.float32)


def dot_nn(a, b):
    return lax.dot_general(a, b, (((1,), (0,)), ((), ())), preferred_element_type=jnp.float32)


def dot_tn(a, b):
    return lax.dot_general(a, b, (((0,), (0,)), ((), ())), preferred_element_type=jnp.float32)


def chip_device(chip, core):
    return {"ctx": 2 * chip + core}


def greet(devices):
    barrier = pltpu.get_barrier_semaphore()
    for there, device in devices:

        @pl.when(there)
        def _():
            pl.semaphore_signal(
                barrier, inc=1, device_id=device, device_id_type=pl.DeviceIdType.MESH
            )

    count = sum(there.astype(jnp.int32) for there, device in devices)
    pl.semaphore_wait(barrier, count)


def remote(source, target, send_sem, recv_sem, device):
    return pltpu.make_async_remote_copy(
        src_ref=source,
        dst_ref=target,
        send_sem=send_sem,
        recv_sem=recv_sem,
        device_id=device,
        device_id_type=pl.DeviceIdType.MESH,
    )


def gather_kernel(
    k_ref,
    v_ref,
    q_ref,
    g_ref,
    kv_ref,
    own_sem,
    line_send,
    line_recv,
    twin_send,
    twin_recv,
    swap_send,
    swap_recv,
):
    me = lax.axis_index("ctx")
    head_width = k_ref.shape[1]
    heads = q_ref.shape[1] // head_width // 2
    chips = (kv_ref.shape[0] - 2 * heads) // 4
    chip, core = me // 2, me % 2
    twin = chip_device(chip, 1 - core)
    has = (chip < chips - 1, chip > 0)
    ahead = (chip_device(chip + 1, core), chip_device(chip - 1, core))
    always = chip >= 0
    greet([(always, twin), (has[0], ahead[0]), (has[1], ahead[1])])

    sources = (k_ref, v_ref)
    own = [
        pltpu.make_async_copy(ref, kv_ref.at[2 * me + part], own_sem.at[part])
        for part, ref in enumerate(sources)
    ]

    def shard_at(way, step):
        return 2 * (chip - step if way == 0 else chip + step) + core

    def along(way, step, hop, part):
        place = kv_ref.at[2 * shard_at(way, step) + part]
        return remote(
            sources[part] if hop == 0 and step == 0 else place,
            place,
            line_send.at[way, hop, part],
            line_recv.at[way, hop, part],
            ahead[way],
        )

    def across(way, step, part):
        place = kv_ref.at[2 * shard_at(way, step) + part]
        return remote(
            sources[part] if step == 0 else place,
            place,
            twin_send.at[way, step, part],
            twin_recv.at[way, step, part],
            twin,
        )

    def arriving(way, step):
        return chip - step >= 0 if way == 0 else chip + step < chips

    for part in range(2):
        for way in range(2):

            @pl.when(has[way])
            def _():
                along(way, 0, 0, part).start()

    for part in range(2):
        across(0, 0, part).start()
        own[part].start()
    swaps = []
    for index, ref in enumerate((q_ref, g_ref)):
        for h in range(heads):
            first = pl.multiple_of(((1 - core) * heads + h) * head_width, head_width)
            swaps.append(
                remote(
                    ref.at[:, pl.ds(first, head_width)],
                    kv_ref.at[4 * chips + index * heads + h],
                    swap_send.at[index, h],
                    swap_recv.at[index, h],
                    twin,
                )
            )
    for copy in swaps:
        copy.start()
    for step in range(1, chips):
        for part in range(2):
            for way in range(2):

                @pl.when(arriving(way, step))
                def _():
                    along(way, step, step - 1, part).wait_recv()

                    @pl.when(has[way])
                    def _():
                        along(way, step, step, part).start()

                    across(way, step, part).start()

    for copy in swaps:
        copy.wait()
    for part in range(2):
        own[part].wait()
        across(0, 0, part).wait()
        for way in range(2):

            @pl.when(has[way])
            def _():
                along(way, 0, 0, part).wait_send()

    for step in range(1, chips):
        for part in range(2):
            for way in range(2):

                @pl.when(arriving(way, step))
                def _():
                    across(way, step, part).wait()

                    @pl.when(has[way])
                    def _():
                        along(way, step, step, part).wait_send()


def gather(keys, values, queries, out_grad):
    rows, width = queries.shape
    n_ctx = lax.axis_size("ctx")
    chips = n_ctx // 2
    heads = width // keys.shape[1] // 2
    return pl.pallas_call(
        gather_kernel,
        out_shape=jax.ShapeDtypeStruct((2 * n_ctx + 2 * heads,) + keys.shape, keys.dtype),
        in_specs=[pl.BlockSpec(memory_space=pl.ANY)] * 4,
        out_specs=pl.BlockSpec(memory_space=pl.ANY),
        scratch_shapes=[
            pltpu.SemaphoreType.DMA((2,)),
            pltpu.SemaphoreType.DMA((2, chips, 2)),
            pltpu.SemaphoreType.DMA((2, chips, 2)),
            pltpu.SemaphoreType.DMA((2, chips, 2)),
            pltpu.SemaphoreType.DMA((2, chips, 2)),
            pltpu.SemaphoreType.DMA((2, heads)),
            pltpu.SemaphoreType.DMA((2, heads)),
        ],
        compiler_params=pltpu.CompilerParams(collective_id=0, has_side_effects=True),
        name="gather_blocks",
    )(keys, values, queries, out_grad)


def reduce_kernel(
    dq_ref,
    dkv_ref,
    q_in_ref,
    kv_in_ref,
    mine_ref,
    twin_ref,
    line_ref,
    sum_ref,
    twin_send,
    twin_recv,
    line_send,
    line_recv,
    query_send,
    query_recv,
    last_send,
    last_recv,
    mine_sem,
):
    me = lax.axis_index("ctx")
    stage = lax.axis_index("pipe")
    stages = lax.axis_size("pipe")
    chips = dkv_ref.shape[0] // 2
    half = dq_ref.shape[2]
    chip, core = me // 2, me % 2
    twin = chip_device(chip, 1 - core)
    has = (chip < chips - 1, chip > 0)
    ahead = (chip_device(chip + 1, core), chip_device(chip - 1, core))
    always = chip >= 0
    before = lax.rem(stage + stages - 1, stages)
    after = lax.rem(stage + 1, stages)

    def own_part(z):
        return pltpu.make_async_copy(dkv_ref.at[2 * z + core], mine_ref.at[z], mine_sem.at[z])

    order = []
    for z in range(chips // 2):
        order += [z, chips - 1 - z]
    for z in order:
        own_part(z).start()
    greet(
        [(always, twin), (has[0], ahead[0]), (has[1], ahead[1])]
        + [
            (always, {"pipe": other, "ctx": 2 * chip + k})
            for other in (before, after)
            for k in range(2)
        ]
    )

    def crossing(z):
        return remote(
            dkv_ref.at[2 * z + 1 - core], twin_ref.at[z], twin_send.at[z], twin_recv.at[z], twin
        )

    for z in order[:2]:
        crossing(z).start()

    lanes = pl.ds(pl.multiple_of(core * half, half), half)

    def query_copy(k, recv_index):
        return remote(
            dq_ref.at[k],
            q_in_ref.at[:, lanes],
            query_send.at[k],
            query_recv.at[recv_index],
            {"pipe": before, "ctx": 2 * chip + k},
        )

    for k in range(2):
        query_copy(k, core).start()
    for z in order[2:]:
        crossing(z).start()

    def passing(way, z, part):
        return remote(
            sum_ref.at[z, part],
            line_ref.at[way, z, part],
            line_send.at[way, z, part],
            line_recv.at[way, z, part],
            ahead[way],
        )

    def add_up(z, part, ways):
        total = mine_ref[z, part].astype(jnp.float32) + twin_ref[z, part].astype(
            jnp.float32
        )
        for way in ways:
            total += line_ref[way, z, part].astype(jnp.float32)
        sum_ref[z, part] = total.astype(sum_ref.dtype)

    for t in range(chips - 1):
        for part in range(2):
            for way in range(2):
                z = chips - 1 - (t - chip) if way == 0 else t - (chips - 1 - chip)
                beyond = (z <= chips - 1) & (z > chip) if way == 0 else (z >= 0) & (z < chip)

                @pl.when(beyond)
                def _():
                    if part == 0:
                        own_part(z).wait()
                        crossing(z).wait_recv()

                    @pl.when(has[1 - way])
                    def _():
                        passing(way, z, part).wait_recv()
                        add_up(z, part, (way,))

                    @pl.when(jnp.logical_not(has[1 - way]))
                    def _():
                        add_up(z, part, ())

                    passing(way, z, part).start()

    own_part(chip).wait()
    crossing(chip).wait_recv()
    lasts = []
    for part in range(2):

        @pl.when(has[0] & has[1])
        def _():
            for way in range(2):
                passing(way, chip, part).wait_recv()
            add_up(chip, part, (0, 1))

        for way in range(2):

            @pl.when(jnp.logical_not(has[way]))
            def _():
                passing(way, chip, part).wait_recv()
                add_up(chip, part, (way,))

        lasts.append(
            remote(
                sum_ref.at[chip, part],
                kv_in_ref.at[part],
                last_send.at[part],
                last_recv.at[part],
                {"pipe": before, "ctx": me},
            )
        )
        lasts[-1].start()
    for k in range(2):
        query_copy(k, k).wait()
    for z in range(chips):
        crossing(z).wait_send()
        for part in range(2):

            @pl.when(z > chip)
            def _():
                passing(0, z, part).wait_send()

            @pl.when(z < chip)
            def _():
                passing(1, z, part).wait_send()

    for copy in lasts:
        copy.wait()


def reduce_and_pass(dq, dkv):
    rows, half = dq.shape[1:]
    n_ctx, _, _, head_width = dkv.shape
    chips = n_ctx // 2
    part = dkv.shape[1:]
    return pl.pallas_call(
        reduce_kernel,
        out_shape=(
            jax.ShapeDtypeStruct((rows, 2 * half), dq.dtype),
            jax.ShapeDtypeStruct((2, rows, head_width), dq.dtype),
        ),
        in_specs=[pl.BlockSpec(memory_space=pl.ANY)] * 2,
        out_specs=(pl.BlockSpec(memory_space=pl.ANY),) * 2,
        scratch_shapes=[
            pltpu.VMEM((chips,) + part, dkv.dtype),
            pltpu.VMEM((chips,) + part, dkv.dtype),
            pltpu.VMEM((2, chips) + part, dkv.dtype),
            pltpu.VMEM((chips,) + part, dkv.dtype),
            pltpu.SemaphoreType.DMA((chips,)),
            pltpu.SemaphoreType.DMA((chips,)),
            pltpu.SemaphoreType.DMA((2, chips, 2)),
            pltpu.SemaphoreType.DMA((2, chips, 2)),
            pltpu.SemaphoreType.DMA((2,)),
            pltpu.SemaphoreType.DMA((2,)),
            pltpu.SemaphoreType.DMA((2,)),
            pltpu.SemaphoreType.DMA((2,)),
            pltpu.SemaphoreType.DMA((chips,)),
        ],
        compiler_params=pltpu.CompilerParams(
            collective_id=1, has_side_effects=True, vmem_limit_bytes=16 * 1024 * 1024
        ),
        name="reduce_and_pass",
    )(dq, dkv)


def attention_kernel(
    sizes_ref,
    placing_ref,
    q_ref,
    g_ref,
    kv_ref,
    dq_ref,
    dkv_ref,
    qs_ref,
    gs_ref,
    s_ref,
    dp_ref,
    top_ref,
    total_ref,
    weighted_ref,
    logsum_ref,
    delta_ref,
    *rest,
):
    low_refs = (rest[:2], rest[2:4])
    dq_acc_ref, acc_ref, place_ref = rest[4:]
    block = q_ref.shape[0] // 2
    head_width = kv_ref.shape[2]
    head_count = q_ref.shape[1] // head_width
    n_ctx = placing_ref.shape[1]
    n_chips = n_ctx // 2
    n_docs = sizes_ref.shape[1]
    heads = head_count // 2
    wide = heads * block
    scale = 1.0 / math.sqrt(head_width)
    scale2 = scale * math.log2(math.e)
    me = lax.axis_index("ctx")
    chip, core = me // 2, me % 2

    starts = [jnp.int32(0)]
    for d in range(n_docs - 1):
        starts.append(starts[-1] + sizes_ref[0, d])
    for d in range(n_ctx):
        low = placing_ref[0, d]
        place_ref[low] = 2 * d
        place_ref[2 * n_ctx - 1 - low] = 2 * d + 1
    acc_ref[...] = jnp.zeros_like(acc_ref)

    def one_strip(step, carry):
        owner = step // 2
        slot = step % 2
        placed = placing_ref[0, 2 * chip + owner]
        query_block = jnp.where(slot == 0, placed, 2 * n_ctx - 1 - placed)
        rows = pl.ds(pl.multiple_of(slot * block, block), block)

        @pl.when(owner == core)
        def _():
            for h in range(heads):
                lanes = pl.ds(
                    pl.multiple_of((core * heads + h) * head_width, head_width), head_width
                )
                qs_ref[h * block : (h + 1) * block, :] = q_ref[rows, lanes]
                gs_ref[h * block : (h + 1) * block, :] = g_ref[rows, lanes]

        @pl.when(owner != core)
        def _():
            for h in range(heads):
                qs_ref[h * block : (h + 1) * block, :] = kv_ref[4 * n_chips + h, rows, :]
                gs_ref[h * block : (h + 1) * block, :] = kv_ref[4 * n_chips + heads + h, rows, :]

        first = query_block * block
        query_pos = first + lax.broadcasted_iota(jnp.int32, (1, block), 1)
        doc_first = jnp.zeros((1, block), jnp.int32)
        strip_first = jnp.int32(0)
        for start in starts[1:]:
            doc_first = jnp.where(query_pos >= start, start, doc_first)
            strip_first = jnp.where(first >= start, start, strip_first)
        low_block = strip_first // block
        tiles = query_block - low_block + 1
        dq_acc_ref[...] = jnp.zeros_like(dq_acc_ref)

        last_doc = jnp.int32(0)
        for start in starts[1:]:
            last_doc = jnp.where(first + block - 1 >= start, start, last_doc)
        top_ref[...] = jnp.full(top_ref.shape, masked_score, jnp.float32)
        total_ref[...] = jnp.zeros_like(total_ref)
        weighted_ref[...] = jnp.zeros_like(weighted_ref)

        def tile_of(t, part):
            stored = place_ref[low_block + t]
            key_rows = pl.ds(pl.multiple_of(stored % 2 * block, block), block)
            return kv_ref[stored // 2 * 2 + part, key_rows, :]

        def fold(x, combine):
            return combine(x.reshape(block // 8, 8, block), axis=0)

        def forward(tiles_now, masked):
            allowed, key_tiles, value_tiles = [], [], []
            for t in tiles_now:
                key_tiles.append(tile_of(t, 0))
                value_tiles.append(tile_of(t, 1))
                if masked:
                    key_pos = (low_block + t) * block + lax.broadcasted_iota(
                        jnp.int32, (block, block), 0
                    )
                    allowed.append((key_pos <= query_pos) & (key_pos >= doc_first))
            tops = []
            for h in range(heads):
                lanes = slice(h * block, (h + 1) * block)
                top = top_ref[:, lanes]
                for i, t in enumerate(tiles_now):
                    scores = dot_nt(key_tiles[i], qs_ref[lanes, :]) * scale2
                    if masked:
                        scores = jnp.where(allowed[i], scores, masked_score)
                    s_ref[t, :, lanes] = scores
                    top = jnp.maximum(top, jnp.max(fold(scores, jnp.max), axis=0, keepdims=True))
                tops.append(top)
            for h in range(heads):
                lanes = slice(h * block, (h + 1) * block)
                factor = jnp.exp2(top_ref[:, lanes] - tops[h])
                top_ref[:, lanes] = tops[h]
                total = total_ref[:, lanes] * factor
                weighted = weighted_ref[:, lanes] * factor
                for i, t in enumerate(tiles_now):
                    grad_probs = dot_nt(value_tiles[i], gs_ref[lanes, :])
                    dp_ref[t, :, lanes] = grad_probs
                    probs = jnp.exp2(s_ref[t, :, lanes] - tops[h])
                    total += fold(probs, jnp.sum)
                    weighted += fold(probs * grad_probs, jnp.sum)
                total_ref[:, lanes] = total
                weighted_ref[:, lanes] = weighted

        def forward_guarded(tiles_now):
            partial = tiles_now[-1] == tiles - 1
            partial |= (low_block + tiles_now[0]) * block < last_doc

            @pl.when(partial)
            def _():
                forward(tiles_now, True)

            @pl.when(jnp.logical_not(partial))
            def _():
                forward(tiles_now, False)

        def backward(tiles_now):
            for i, t in enumerate(tiles_now):
                stored = place_ref[low_block + t]
                key_rows = pl.ds(pl.multiple_of(stored % 2 * block, block), block)
                key_tile = tile_of(t, 0)
                for h in range(heads):
                    lanes = slice(h * block, (h + 1) * block)
                    for r in range(0, block, 64):
                        softmax = jnp.exp2(s_ref[t, r : r + 64, lanes] - logsum_ref[:, lanes])
                        grad_scores = softmax * (dp_ref[t, r : r + 64, lanes] - delta_ref[:, lanes])
                        low_refs[i][0][r : r + 64, lanes] = softmax.astype(jnp.bfloat16)
                        low_refs[i][1][r : r + 64, lanes] = grad_scores.astype(jnp.bfloat16)
                acc_ref[stored // 2, 1, key_rows, :] += dot_nn(low_refs[i][0][...], gs_ref[...])
                acc_ref[stored // 2, 0, key_rows, :] += dot_nn(low_refs[i][1][...], qs_ref[...])
                dq_acc_ref[...] += dot_tn(low_refs[i][1][...], key_tile)

        def over_tiles(work):
            def pair(i, carry):
                work([2 * i, 2 * i + 1])
                return carry

            lax.fori_loop(0, tiles // 2, pair, 0)

            @pl.when(tiles % 2 == 1)
            def _():
                work([tiles - 1])

        over_tiles(forward_guarded)
        total = jnp.sum(total_ref[...], axis=0, keepdims=True)
        logsum_ref[...] = top_ref[...] + jnp.log2(total)
        delta_ref[...] = jnp.sum(weighted_ref[...], axis=0, keepdims=True) / total
        over_tiles(backward)
        for h in range(heads):
            dq_ref[owner, rows, h * head_width : (h + 1) * head_width] = (
                dq_acc_ref[h * block : (h + 1) * block, :] * scale
            ).astype(jnp.bfloat16)
        return carry

    lax.fori_loop(0, 4, one_strip, 0)
    dkv_ref[:, 0] = (acc_ref[:, 0] * scale).astype(dkv_ref.dtype)
    dkv_ref[:, 1] = acc_ref[:, 1].astype(dkv_ref.dtype)


def attention_backward(doc_lengths, assignment, queries, out_grad, kv):
    rows, width = queries.shape
    n_ctx = assignment.shape[1]
    length = n_ctx * rows
    block = rows // 2
    head_width = kv.shape[2]
    wide = width // head_width // 2 * block
    most = length // 2
    tiles = most // block + 1
    strips = 2 * tiles * block * wide * 4
    limit = strips + 4 * length * head_width * 4 + 20 * rows * width + 6 * 1024 * 1024
    vmem = pl.BlockSpec(memory_space=pltpu.VMEM)
    smem = pl.BlockSpec(memory_space=pltpu.SMEM)
    return pl.pallas_call(
        attention_kernel,
        out_shape=(
            jax.ShapeDtypeStruct((2, rows, width // 2), jnp.bfloat16),
            jax.ShapeDtypeStruct((n_ctx, 2, rows, head_width), jnp.bfloat16),
        ),
        in_specs=[smem, smem, vmem, vmem, vmem],
        out_specs=(vmem, vmem),
        scratch_shapes=[
            pltpu.VMEM((wide, head_width), jnp.bfloat16),
            pltpu.VMEM((wide, head_width), jnp.bfloat16),
            pltpu.VMEM((tiles, block, wide), jnp.float32),
            pltpu.VMEM((tiles, block, wide), jnp.float32),
            pltpu.VMEM((1, wide), jnp.float32),
            pltpu.VMEM((8, wide), jnp.float32),
            pltpu.VMEM((8, wide), jnp.float32),
            pltpu.VMEM((1, wide), jnp.float32),
            pltpu.VMEM((1, wide), jnp.float32),
            pltpu.VMEM((block, wide), jnp.bfloat16),
            pltpu.VMEM((block, wide), jnp.bfloat16),
            pltpu.VMEM((block, wide), jnp.bfloat16),
            pltpu.VMEM((block, wide), jnp.bfloat16),
            pltpu.VMEM((wide, head_width), jnp.float32),
            pltpu.VMEM((n_ctx, 2, rows, head_width), jnp.float32),
            pltpu.SMEM((2 * assignment.shape[1],), jnp.int32),
        ],
        compiler_params=pltpu.CompilerParams(vmem_limit_bytes=limit),
        name="attention_backward",
    )(doc_lengths, assignment, queries, out_grad, kv)


def local(queries, keys, values, out_grad, doc_lengths, assignment):
    kv = gather(keys[0], values[0], queries[0], out_grad[0])
    dq, dkv = attention_backward(doc_lengths, assignment, queries[0], out_grad[0], kv)
    query_in, kv_in = reduce_and_pass(dq, dkv)
    return query_in[None], kv_in[0][None], kv_in[1][None]


def solution(mesh):
    return jax.shard_map(
        local,
        mesh=mesh,
        in_specs=(
            P("pipe", "ctx", None),
            P("pipe", "ctx", None),
            P("pipe", "ctx", None),
            P("pipe", "ctx", None),
            P("pipe", None),
            P("pipe", None),
        ),
        out_specs=(P("pipe", "ctx", None), P("pipe", "ctx", None), P("pipe", "ctx", None)),
        check_vma=False,
    )
```

```python
import math

import jax
import jax.numpy as jnp
from jax import lax
from jax.experimental import pallas as pl
from jax.experimental.pallas import tpu as pltpu
from jax.sharding import PartitionSpec as P

masked_score = -1e30


def dot_nt(a, b):
    return lax.dot_general(a, b, (((1,), (1,)), ((), ())), preferred_element_type=jnp.float32)


def dot_nn(a, b):
    return lax.dot_general(a, b, (((1,), (0,)), ((), ())), preferred_element_type=jnp.float32)


def dot_tn(a, b):
    return lax.dot_general(a, b, (((0,), (0,)), ((), ())), preferred_element_type=jnp.float32)


def chip_device(chip, core):
    return {"ctx": 2 * chip + core}


def greet(devices):
    barrier = pltpu.get_barrier_semaphore()
    for there, device in devices:

        @pl.when(there)
        def _():
            pl.semaphore_signal(
                barrier, inc=1, device_id=device, device_id_type=pl.DeviceIdType.MESH
            )

    count = sum(there.astype(jnp.int32) for there, device in devices)
    pl.semaphore_wait(barrier, count)


def remote(source, target, send_sem, recv_sem, device):
    return pltpu.make_async_remote_copy(
        src_ref=source,
        dst_ref=target,
        send_sem=send_sem,
        recv_sem=recv_sem,
        device_id=device,
        device_id_type=pl.DeviceIdType.MESH,
    )


def gather_kernel(
    k_ref,
    v_ref,
    q_ref,
    g_ref,
    kv_ref,
    own_sem,
    line_send,
    line_recv,
    twin_send,
    twin_recv,
    swap_send,
    swap_recv,
):
    me = lax.axis_index("ctx")
    head_width = k_ref.shape[1]
    heads = q_ref.shape[1] // head_width // 2
    chips = (kv_ref.shape[0] - 2 * heads) // 4
    chip, core = me // 2, me % 2
    twin = chip_device(chip, 1 - core)
    has = (chip < chips - 1, chip > 0)
    ahead = (chip_device(chip + 1, core), chip_device(chip - 1, core))
    always = chip >= 0
    greet([(always, twin), (has[0], ahead[0]), (has[1], ahead[1])])

    sources = (k_ref, v_ref)
    own = [
        pltpu.make_async_copy(ref, kv_ref.at[2 * me + part], own_sem.at[part])
        for part, ref in enumerate(sources)
    ]

    def shard_at(way, step):
        return 2 * (chip - step if way == 0 else chip + step) + core

    def along(way, step, hop, part):
        place = kv_ref.at[2 * shard_at(way, step) + part]
        return remote(
            sources[part] if hop == 0 and step == 0 else place,
            place,
            line_send.at[way, hop, part],
            line_recv.at[way, hop, part],
            ahead[way],
        )

    def across(way, step, part):
        place = kv_ref.at[2 * shard_at(way, step) + part]
        return remote(
            sources[part] if step == 0 else place,
            place,
            twin_send.at[way, step, part],
            twin_recv.at[way, step, part],
            twin,
        )

    def arriving(way, step):
        return chip - step >= 0 if way == 0 else chip + step < chips

    for part in range(2):
        for way in range(2):

            @pl.when(has[way])
            def _():
                along(way, 0, 0, part).start()

    for part in range(2):
        across(0, 0, part).start()
        own[part].start()
    swaps = []
    for index, ref in enumerate((q_ref, g_ref)):
        for h in range(heads):
            first = pl.multiple_of(((1 - core) * heads + h) * head_width, head_width)
            swaps.append(
                remote(
                    ref.at[:, pl.ds(first, head_width)],
                    kv_ref.at[4 * chips + index * heads + h],
                    swap_send.at[index, h],
                    swap_recv.at[index, h],
                    twin,
                )
            )
    for copy in swaps:
        copy.start()
    for step in range(1, chips):
        for part in range(2):
            for way in range(2):

                @pl.when(arriving(way, step))
                def _():
                    along(way, step, step - 1, part).wait_recv()

                    @pl.when(has[way])
                    def _():
                        along(way, step, step, part).start()

                    across(way, step, part).start()

    for copy in swaps:
        copy.wait()
    for part in range(2):
        own[part].wait()
        across(0, 0, part).wait()
        for way in range(2):

            @pl.when(has[way])
            def _():
                along(way, 0, 0, part).wait_send()

    for step in range(1, chips):
        for part in range(2):
            for way in range(2):

                @pl.when(arriving(way, step))
                def _():
                    across(way, step, part).wait()

                    @pl.when(has[way])
                    def _():
                        along(way, step, step, part).wait_send()


def gather(keys, values, queries, out_grad):
    rows, width = queries.shape
    n_ctx = lax.axis_size("ctx")
    chips = n_ctx // 2
    heads = width // keys.shape[1] // 2
    return pl.pallas_call(
        gather_kernel,
        out_shape=jax.ShapeDtypeStruct((2 * n_ctx + 2 * heads,) + keys.shape, keys.dtype),
        in_specs=[pl.BlockSpec(memory_space=pl.ANY)] * 4,
        out_specs=pl.BlockSpec(memory_space=pl.ANY),
        scratch_shapes=[
            pltpu.SemaphoreType.DMA((2,)),
            pltpu.SemaphoreType.DMA((2, chips, 2)),
            pltpu.SemaphoreType.DMA((2, chips, 2)),
            pltpu.SemaphoreType.DMA((2, chips, 2)),
            pltpu.SemaphoreType.DMA((2, chips, 2)),
            pltpu.SemaphoreType.DMA((2, heads)),
            pltpu.SemaphoreType.DMA((2, heads)),
        ],
        compiler_params=pltpu.CompilerParams(collective_id=0, has_side_effects=True),
        name="gather_blocks",
    )(keys, values, queries, out_grad)


def reduce_kernel(
    dq_ref,
    dkv_ref,
    q_in_ref,
    kv_in_ref,
    mine_ref,
    twin_ref,
    line_ref,
    sum_ref,
    twin_send,
    twin_recv,
    line_send,
    line_recv,
    query_send,
    query_recv,
    last_send,
    last_recv,
    mine_sem,
):
    me = lax.axis_index("ctx")
    stage = lax.axis_index("pipe")
    stages = lax.axis_size("pipe")
    chips = dkv_ref.shape[0] // 2
    half = dq_ref.shape[2]
    chip, core = me // 2, me % 2
    twin = chip_device(chip, 1 - core)
    has = (chip < chips - 1, chip > 0)
    ahead = (chip_device(chip + 1, core), chip_device(chip - 1, core))
    always = chip >= 0
    before = lax.rem(stage + stages - 1, stages)
    after = lax.rem(stage + 1, stages)

    def own_part(z):
        return pltpu.make_async_copy(dkv_ref.at[2 * z + core], mine_ref.at[z], mine_sem.at[z])

    order = []
    for z in range(chips // 2):
        order += [z, chips - 1 - z]
    for z in order:
        own_part(z).start()
    greet(
        [(always, twin), (has[0], ahead[0]), (has[1], ahead[1])]
        + [
            (always, {"pipe": other, "ctx": 2 * chip + k})
            for other in (before, after)
            for k in range(2)
        ]
    )

    def crossing(z):
        return remote(
            dkv_ref.at[2 * z + 1 - core], twin_ref.at[z], twin_send.at[z], twin_recv.at[z], twin
        )

    for z in order[:2]:
        crossing(z).start()

    lanes = pl.ds(pl.multiple_of(core * half, half), half)

    def query_copy(k, recv_index):
        return remote(
            dq_ref.at[k],
            q_in_ref.at[:, lanes],
            query_send.at[k],
            query_recv.at[recv_index],
            {"pipe": before, "ctx": 2 * chip + k},
        )

    for k in range(2):
        query_copy(k, core).start()
    for z in order[2:]:
        crossing(z).start()

    def passing(way, z, part):
        return remote(
            sum_ref.at[z, part],
            line_ref.at[way, z, part],
            line_send.at[way, z, part],
            line_recv.at[way, z, part],
            ahead[way],
        )

    def add_up(z, part, ways):
        total = mine_ref[z, part].astype(jnp.float32) + twin_ref[z, part].astype(
            jnp.float32
        )
        for way in ways:
            total += line_ref[way, z, part].astype(jnp.float32)
        sum_ref[z, part] = total.astype(sum_ref.dtype)

    for t in range(chips - 1):
        for part in range(2):
            for way in range(2):
                z = chips - 1 - (t - chip) if way == 0 else t - (chips - 1 - chip)
                beyond = (z <= chips - 1) & (z > chip) if way == 0 else (z >= 0) & (z < chip)

                @pl.when(beyond)
                def _():
                    if part == 0:
                        own_part(z).wait()
                        crossing(z).wait_recv()

                    @pl.when(has[1 - way])
                    def _():
                        passing(way, z, part).wait_recv()
                        add_up(z, part, (way,))

                    @pl.when(jnp.logical_not(has[1 - way]))
                    def _():
                        add_up(z, part, ())

                    passing(way, z, part).start()

    own_part(chip).wait()
    crossing(chip).wait_recv()
    lasts = []
    for part in range(2):

        @pl.when(has[0] & has[1])
        def _():
            for way in range(2):
                passing(way, chip, part).wait_recv()
            add_up(chip, part, (0, 1))

        for way in range(2):

            @pl.when(jnp.logical_not(has[way]))
            def _():
                passing(way, chip, part).wait_recv()
                add_up(chip, part, (way,))

        lasts.append(
            remote(
                sum_ref.at[chip, part],
                kv_in_ref.at[part],
                last_send.at[part],
                last_recv.at[part],
                {"pipe": before, "ctx": me},
            )
        )
        lasts[-1].start()
    for k in range(2):
        query_copy(k, k).wait()
    for z in range(chips):
        crossing(z).wait_send()
        for part in range(2):

            @pl.when(z > chip)
            def _():
                passing(0, z, part).wait_send()

            @pl.when(z < chip)
            def _():
                passing(1, z, part).wait_send()

    for copy in lasts:
        copy.wait()


def reduce_and_pass(dq, dkv):
    rows, half = dq.shape[1:]
    n_ctx, _, _, head_width = dkv.shape
    chips = n_ctx // 2
    part = dkv.shape[1:]
    return pl.pallas_call(
        reduce_kernel,
        out_shape=(
            jax.ShapeDtypeStruct((rows, 2 * half), dq.dtype),
            jax.ShapeDtypeStruct((2, rows, head_width), dq.dtype),
        ),
        in_specs=[pl.BlockSpec(memory_space=pl.ANY)] * 2,
        out_specs=(pl.BlockSpec(memory_space=pl.ANY),) * 2,
        scratch_shapes=[
            pltpu.VMEM((chips,) + part, dkv.dtype),
            pltpu.VMEM((chips,) + part, dkv.dtype),
            pltpu.VMEM((2, chips) + part, dkv.dtype),
            pltpu.VMEM((chips,) + part, dkv.dtype),
            pltpu.SemaphoreType.DMA((chips,)),
            pltpu.SemaphoreType.DMA((chips,)),
            pltpu.SemaphoreType.DMA((2, chips, 2)),
            pltpu.SemaphoreType.DMA((2, chips, 2)),
            pltpu.SemaphoreType.DMA((2,)),
            pltpu.SemaphoreType.DMA((2,)),
            pltpu.SemaphoreType.DMA((2,)),
            pltpu.SemaphoreType.DMA((2,)),
            pltpu.SemaphoreType.DMA((chips,)),
        ],
        compiler_params=pltpu.CompilerParams(
            collective_id=1, has_side_effects=True, vmem_limit_bytes=16 * 1024 * 1024
        ),
        name="reduce_and_pass",
    )(dq, dkv)


def attention_kernel(
    sizes_ref,
    placing_ref,
    q_ref,
    g_ref,
    kv_ref,
    dq_ref,
    dkv_ref,
    qs_ref,
    gs_ref,
    s_ref,
    dp_ref,
    top_ref,
    total_ref,
    weighted_ref,
    logsum_ref,
    delta_ref,
    *rest,
):
    low_refs = (rest[:2], rest[2:4])
    dq_acc_ref, acc_ref, place_ref = rest[4:]
    block = q_ref.shape[0] // 2
    head_width = kv_ref.shape[2]
    head_count = q_ref.shape[1] // head_width
    n_ctx = placing_ref.shape[1]
    n_chips = n_ctx // 2
    n_docs = sizes_ref.shape[1]
    heads = head_count // 2
    wide = heads * block
    scale = 1.0 / math.sqrt(head_width)
    scale2 = scale * math.log2(math.e)
    me = lax.axis_index("ctx")
    chip, core = me // 2, me % 2

    starts = [jnp.int32(0)]
    for d in range(n_docs - 1):
        starts.append(starts[-1] + sizes_ref[0, d])
    for d in range(n_ctx):
        low = placing_ref[0, d]
        place_ref[low] = 2 * d
        place_ref[2 * n_ctx - 1 - low] = 2 * d + 1
    acc_ref[...] = jnp.zeros_like(acc_ref)

    def one_strip(step, carry):
        owner = step // 2
        slot = step % 2
        placed = placing_ref[0, 2 * chip + owner]
        query_block = jnp.where(slot == 0, placed, 2 * n_ctx - 1 - placed)
        rows = pl.ds(pl.multiple_of(slot * block, block), block)

        @pl.when(owner == core)
        def _():
            for h in range(heads):
                lanes = pl.ds(
                    pl.multiple_of((core * heads + h) * head_width, head_width), head_width
                )
                qs_ref[h * block : (h + 1) * block, :] = q_ref[rows, lanes]
                gs_ref[h * block : (h + 1) * block, :] = g_ref[rows, lanes]

        @pl.when(owner != core)
        def _():
            for h in range(heads):
                qs_ref[h * block : (h + 1) * block, :] = kv_ref[4 * n_chips + h, rows, :]
                gs_ref[h * block : (h + 1) * block, :] = kv_ref[4 * n_chips + heads + h, rows, :]

        first = query_block * block
        query_pos = first + lax.broadcasted_iota(jnp.int32, (1, block), 1)
        doc_first = jnp.zeros((1, block), jnp.int32)
        strip_first = jnp.int32(0)
        for start in starts[1:]:
            doc_first = jnp.where(query_pos >= start, start, doc_first)
            strip_first = jnp.where(first >= start, start, strip_first)
        low_block = strip_first // block
        tiles = query_block - low_block + 1
        dq_acc_ref[...] = jnp.zeros_like(dq_acc_ref)

        last_doc = jnp.int32(0)
        for start in starts[1:]:
            last_doc = jnp.where(first + block - 1 >= start, start, last_doc)
        top_ref[...] = jnp.full(top_ref.shape, masked_score, jnp.float32)
        total_ref[...] = jnp.zeros_like(total_ref)
        weighted_ref[...] = jnp.zeros_like(weighted_ref)

        def tile_of(t, part):
            stored = place_ref[low_block + t]
            key_rows = pl.ds(pl.multiple_of(stored % 2 * block, block), block)
            return kv_ref[stored // 2 * 2 + part, key_rows, :]

        def fold(x, combine):
            return combine(x.reshape(block // 8, 8, block), axis=0)

        def forward(tiles_now, masked):
            allowed, key_tiles, value_tiles = [], [], []
            for t in tiles_now:
                key_tiles.append(tile_of(t, 0))
                value_tiles.append(tile_of(t, 1))
                if masked:
                    key_pos = (low_block + t) * block + lax.broadcasted_iota(
                        jnp.int32, (block, block), 0
                    )
                    allowed.append((key_pos <= query_pos) & (key_pos >= doc_first))
            tops = []
            for h in range(heads):
                lanes = slice(h * block, (h + 1) * block)
                top = top_ref[:, lanes]
                for i, t in enumerate(tiles_now):
                    scores = dot_nt(key_tiles[i], qs_ref[lanes, :]) * scale2
                    if masked:
                        scores = jnp.where(allowed[i], scores, masked_score)
                    s_ref[t, :, lanes] = scores
                    top = jnp.maximum(top, jnp.max(fold(scores, jnp.max), axis=0, keepdims=True))
                tops.append(top)
            for h in range(heads):
                lanes = slice(h * block, (h + 1) * block)
                factor = jnp.exp2(top_ref[:, lanes] - tops[h])
                top_ref[:, lanes] = tops[h]
                total = total_ref[:, lanes] * factor
                weighted = weighted_ref[:, lanes] * factor
                for i, t in enumerate(tiles_now):
                    grad_probs = dot_nt(value_tiles[i], gs_ref[lanes, :])
                    dp_ref[t, :, lanes] = grad_probs
                    probs = jnp.exp2(s_ref[t, :, lanes] - tops[h])
                    total += fold(probs, jnp.sum)
                    weighted += fold(probs * grad_probs, jnp.sum)
                total_ref[:, lanes] = total
                weighted_ref[:, lanes] = weighted

        def forward_guarded(tiles_now):
            partial = tiles_now[-1] == tiles - 1
            partial |= (low_block + tiles_now[0]) * block < last_doc

            @pl.when(partial)
            def _():
                forward(tiles_now, True)

            @pl.when(jnp.logical_not(partial))
            def _():
                forward(tiles_now, False)

        def backward(tiles_now):
            for i, t in enumerate(tiles_now):
                stored = place_ref[low_block + t]
                key_rows = pl.ds(pl.multiple_of(stored % 2 * block, block), block)
                key_tile = tile_of(t, 0)
                key_part, value_part = 0.0, 0.0
                for h in range(heads):
                    lanes = slice(h * block, (h + 1) * block)
                    for r in range(0, block, 64):
                        softmax = jnp.exp2(s_ref[t, r : r + 64, lanes] - logsum_ref[:, lanes])
                        grad_scores = softmax * (dp_ref[t, r : r + 64, lanes] - delta_ref[:, lanes])
                        low_refs[i][0][r : r + 64, lanes] = softmax.astype(jnp.bfloat16)
                        low_refs[i][1][r : r + 64, lanes] = grad_scores.astype(jnp.bfloat16)
                    if h % 2 == 1:
                        two = slice((h - 1) * block, (h + 1) * block)
                        value_part += dot_nn(low_refs[i][0][:, two], gs_ref[two, :])
                        key_part += dot_nn(low_refs[i][1][:, two], qs_ref[two, :])
                        dq_acc_ref[two, :] += dot_tn(low_refs[i][1][:, two], key_tile)
                acc_ref[stored // 2, 1, key_rows, :] += value_part
                acc_ref[stored // 2, 0, key_rows, :] += key_part

        def over_tiles(work):
            def pair(i, carry):
                work([2 * i, 2 * i + 1])
                return carry

            lax.fori_loop(0, tiles // 2, pair, 0)

            @pl.when(tiles % 2 == 1)
            def _():
                work([tiles - 1])

        over_tiles(forward_guarded)
        total = jnp.sum(total_ref[...], axis=0, keepdims=True)
        logsum_ref[...] = top_ref[...] + jnp.log2(total)
        delta_ref[...] = jnp.sum(weighted_ref[...], axis=0, keepdims=True) / total
        over_tiles(backward)
        for h in range(heads):
            dq_ref[owner, rows, h * head_width : (h + 1) * head_width] = (
                dq_acc_ref[h * block : (h + 1) * block, :] * scale
            ).astype(jnp.bfloat16)
        return carry

    lax.fori_loop(0, 4, one_strip, 0)
    dkv_ref[:, 0] = (acc_ref[:, 0] * scale).astype(dkv_ref.dtype)
    dkv_ref[:, 1] = acc_ref[:, 1].astype(dkv_ref.dtype)


def attention_backward(doc_lengths, assignment, queries, out_grad, kv):
    rows, width = queries.shape
    n_ctx = assignment.shape[1]
    length = n_ctx * rows
    block = rows // 2
    head_width = kv.shape[2]
    wide = width // head_width // 2 * block
    most = length // 2
    tiles = most // block + 1
    strips = 2 * tiles * block * wide * 4
    limit = strips + 4 * length * head_width * 4 + 20 * rows * width + 6 * 1024 * 1024
    vmem = pl.BlockSpec(memory_space=pltpu.VMEM)
    smem = pl.BlockSpec(memory_space=pltpu.SMEM)
    return pl.pallas_call(
        attention_kernel,
        out_shape=(
            jax.ShapeDtypeStruct((2, rows, width // 2), jnp.bfloat16),
            jax.ShapeDtypeStruct((n_ctx, 2, rows, head_width), jnp.bfloat16),
        ),
        in_specs=[smem, smem, vmem, vmem, vmem],
        out_specs=(vmem, vmem),
        scratch_shapes=[
            pltpu.VMEM((wide, head_width), jnp.bfloat16),
            pltpu.VMEM((wide, head_width), jnp.bfloat16),
            pltpu.VMEM((tiles, block, wide), jnp.float32),
            pltpu.VMEM((tiles, block, wide), jnp.float32),
            pltpu.VMEM((1, wide), jnp.float32),
            pltpu.VMEM((8, wide), jnp.float32),
            pltpu.VMEM((8, wide), jnp.float32),
            pltpu.VMEM((1, wide), jnp.float32),
            pltpu.VMEM((1, wide), jnp.float32),
            pltpu.VMEM((block, wide), jnp.bfloat16),
            pltpu.VMEM((block, wide), jnp.bfloat16),
            pltpu.VMEM((block, wide), jnp.bfloat16),
            pltpu.VMEM((block, wide), jnp.bfloat16),
            pltpu.VMEM((wide, head_width), jnp.float32),
            pltpu.VMEM((n_ctx, 2, rows, head_width), jnp.float32),
            pltpu.SMEM((2 * assignment.shape[1],), jnp.int32),
        ],
        compiler_params=pltpu.CompilerParams(vmem_limit_bytes=limit),
        name="attention_backward",
    )(doc_lengths, assignment, queries, out_grad, kv)


def local(queries, keys, values, out_grad, doc_lengths, assignment):
    kv = gather(keys[0], values[0], queries[0], out_grad[0])
    dq, dkv = attention_backward(doc_lengths, assignment, queries[0], out_grad[0], kv)
    query_in, kv_in = reduce_and_pass(dq, dkv)
    return query_in[None], kv_in[0][None], kv_in[1][None]


def solution(mesh):
    return jax.shard_map(
        local,
        mesh=mesh,
        in_specs=(
            P("pipe", "ctx", None),
            P("pipe", "ctx", None),
            P("pipe", "ctx", None),
            P("pipe", "ctx", None),
            P("pipe", None),
            P("pipe", None),
        ),
        out_specs=(P("pipe", "ctx", None), P("pipe", "ctx", None), P("pipe", "ctx", None)),
        check_vma=False,
    )
```
